32 devices in a mesh: groups: 2 (over y), ctx: 4 (over z), dp: 4 (over x, core).
Axes of the slice: x: 2, y: 2, z: 4, core: 2. Of those that a mesh axis runs over, the one named last changes fastest.
Arguments:
- resid: bfloat16 [8, 512, 1024], P(('groups', 'dp'), 'ctx'), parts along dimension 0, may hold values from -3 to 3
- query: bfloat16 [8, 512, 512], P(('groups', 'dp'), 'ctx'), parts along dimension 0, may hold values from -48 to 48, as said below
- keys: bfloat16 [8, 512, 512], P(('groups', 'dp'), 'ctx'), parts along dimension 0, may hold values from -48 to 48, as said below
- values: bfloat16 [8, 512, 512], P(('groups', 'dp'), 'ctx'), parts along dimension 0, may hold values from -6 to 6
- w_out: bfloat16 [512, 1024], replicated, may hold values from -0.25 to 0.25
- norm_gain: float32 [1024], replicated, may hold values from 0.5 to 1.5
- w_in: bfloat16 [1024, 1024], replicated, may hold values from -0.1875 to 0.1875
- kernel: float32 [31, 512], replicated, may hold values from -1 to 1
- conv_gain: float32 [512], replicated, may hold values from 0.5 to 1.5
- conv_bias: float32 [512], replicated, may hold values from -3 to 3
- cotangent: bfloat16 [8, 512, 512], P(('groups', 'dp'), 'ctx'), parts along dimension 0, may hold values from -6 to 6
Outputs:
- conv_act: bfloat16 [8, 512, 512], P(('groups', 'dp'), 'ctx'), parts along dimension 0
- d_hidden: bfloat16 [8, 512, 1024], P(('groups', 'dp'), 'ctx'), parts along dimension 0
- d_kernel: float32 [62, 512], P('groups'), parts along dimension 0
- d_conv_gain: float32 [1024], P('groups'), parts along dimension 0
- d_conv_bias: float32 [1024], P('groups'), parts along dimension 0
The draws below stay inside these ranges and needn't reach their ends.
There are 2 independent parts, one for each index of `groups`. The reference program is written for one: setup_inputs(seed, part) draws one part's arguments, and reference() takes and returns one part's arrays. A program takes and returns all parts, laid end to end along the dimension named above; an argument that names none is the same for every part. Nothing has to cross between parts.
Inputs may be any that keep to these rules, and one draw needn't show every extreme that they name: `query`: queries of 8 heads of 64 features, side by side. `keys`: keys of 8 heads of 64 features, side by side.
All inputs are finite; a program needn't handle non-finite values.
Results may differ from the reference program's by a relative error of at most 0.015.
Values may be sent and summed in bfloat16 or wider, within the bound.
No kernel may reach another device: no remote copies, remote signals or barrier semaphores. Data moves between devices by JAX's collectives and lax.ppermute only.
A program may use at most 64 MiB of HBM per device.

```python
import math
import jax
import jax.numpy as jnp
from jax import lax

D = 1024
HEADS = 8
HEAD_DIM = 64
CH = 512
TAPS = 31
POOL = 4
FRAMES = 128
LENGTH = 512
KEYLEN = 128
RECS = 4


def drawn_pair(key):
    base_key = jax.random.fold_in(key, 11)
    key_first, key_second = jax.random.split(base_key)
    full_shape = (RECS, LENGTH, HEADS * HEAD_DIM)
    keys_raw = jnp.clip(jax.random.normal(key_first, full_shape, jnp.float32), -4.0, 4.0)
    query_base = jnp.clip(jax.random.normal(key_second, full_shape, jnp.float32), -4.0, 4.0)
    return (2.5 * query_base, keys_raw)


def draw_query(key, part):
    return drawn_pair(key)[0].astype(jnp.bfloat16)


def draw_keys(key, part):
    return drawn_pair(key)[1].astype(jnp.bfloat16)


def levels(stream_key, extent, shards, smallest, high):
    level = 1.0
    for dim, parts in shards:
        draws = jax.random.uniform(jax.random.fold_in(jax.random.fold_in(stream_key, 6), dim), (parts,), jnp.float32, smallest / len(shards), high / len(shards))
        level = level * jnp.repeat(jnp.exp(draws), extent[dim] // parts).reshape((-1,) + (1,) * (len(extent) - 1 - dim))
    return level


def gaussian(key, dims, deviation, bound, shards=(), kind=jnp.bfloat16):
    loudness = levels(key, dims, shards, -0.22, 0.18) if shards else 1.0
    values = jax.random.normal(key, dims, jnp.float32) * deviation * loudness
    return jnp.minimum(jnp.maximum(values, -bound), bound).astype(kind)


def setup_inputs(seed: int = 0, part: int = 0) -> dict:
    key_of = jax.random.split(jax.random.key(seed), 12)
    part_splits = jax.random.split(jax.random.fold_in(key_of[11], part), 12)
    return {
        "resid": gaussian(part_splits[0], (RECS, LENGTH, D), 0.5, 3.0, ((0, 4), (1, 4))),
        "query": draw_query(jax.random.fold_in(jax.random.fold_in(key_of[11], part), 71), part),
        "keys": draw_keys(jax.random.fold_in(jax.random.fold_in(key_of[11], part), 71), part),
        "values": gaussian(part_splits[3], (RECS, LENGTH, HEADS * HEAD_DIM), 1.0, 6.0, ((0, 4), (1, 4))),
        "w_out": gaussian(key_of[4], (HEADS * HEAD_DIM, D), (HEADS * HEAD_DIM) ** -0.5, 0.25),
        "norm_gain": jnp.clip(1.0 + 0.1 * jax.random.normal(key_of[5], (D,), jnp.float32), 0.5, 1.5),
        "w_in": gaussian(key_of[6], (D, 2 * CH), D ** -0.5, 0.1875),
        "kernel": gaussian(key_of[7], (TAPS, CH), TAPS ** -0.5, 1.0, (), jnp.float32),
        "conv_gain": jnp.clip(1.0 + 0.1 * jax.random.normal(key_of[8], (CH,), jnp.float32), 0.5, 1.5),
        "conv_bias": gaussian(key_of[9], (CH,), 0.5, 3.0, (), jnp.float32),
        "cotangent": gaussian(part_splits[10], (RECS, LENGTH, CH), 1.0, 6.0, ((0, 4), (1, 4))),
    }


EPSILON = 1e-05

def layer_stats(values_in):
    average = lax.optimization_barrier(jnp.mean(values_in, axis=-1, keepdims=True))
    centred = values_in - average
    inv_std = lax.rsqrt(lax.optimization_barrier(jnp.mean(centred * centred, axis=-1, keepdims=True)) + EPSILON)
    return (centred * inv_std, inv_std)

def norm_back(grad_norm, normal, inv_std):
    return inv_std * (grad_norm - lax.optimization_barrier(jnp.mean(grad_norm, axis=-1, keepdims=True)) - normal * lax.optimization_barrier(jnp.mean(grad_norm * normal, axis=-1, keepdims=True)))

def depthwise(padded, kernel, length):
    summed = jnp.zeros(padded.shape[:1] + (length,) + padded.shape[2:], jnp.float32)
    for tap_index in range(kernel.shape[0]):
        summed = summed + kernel[tap_index] * padded[:, tap_index:tap_index + length].astype(jnp.float32)
    return summed

def conv_tail(conv_out, cotangent, conv_gain, conv_bias):
    z_normed, inv_std = layer_stats(conv_out)
    act_in = z_normed * conv_gain + conv_bias
    sig_act = jax.nn.sigmoid(act_in)
    conv_act = (act_in * sig_act).astype(jnp.bfloat16)
    d_act = cotangent.astype(jnp.float32) * (sig_act + act_in * sig_act * (1.0 - sig_act))
    d_conv = norm_back(d_act * conv_gain, z_normed, inv_std).astype(jnp.bfloat16)
    return (conv_act, d_act, z_normed, d_conv)

def pool_frames(array_in):
    shaped = array_in.astype(jnp.float32).reshape(array_in.shape[0] // POOL, POOL, array_in.shape[1])
    return lax.optimization_barrier(jnp.mean(shaped, axis=1)).astype(jnp.bfloat16)

def reference(resid, query, keys, values, w_out, norm_gain, w_in, kernel, conv_gain, conv_bias, cotangent):
    score_scale = 1.0 / math.sqrt(HEAD_DIM)

    def one_record(items):
        query_rec, keys_rec, values_rec = items
        key_heads = pool_frames(keys_rec).astype(jnp.float32).reshape(KEYLEN, HEADS, HEAD_DIM)
        value_heads = pool_frames(values_rec).astype(jnp.float32).reshape(KEYLEN, HEADS, HEAD_DIM)
        query_blocks = query_rec.astype(jnp.float32).reshape(LENGTH // FRAMES, FRAMES, HEADS, HEAD_DIM)

        def query_block(block_rows):
            scores = jnp.einsum('qhd,khd->hqk', block_rows, key_heads) * score_scale
            row_max = lax.optimization_barrier(jnp.max(scores, axis=2, keepdims=True))
            exp_scores = jnp.exp(scores - row_max)
            totals = lax.optimization_barrier(jnp.sum(exp_scores, axis=2))
            probs = lax.optimization_barrier(exp_scores.astype(jnp.bfloat16)).astype(jnp.float32)
            weighted = jnp.einsum('hqk,khd->qhd', probs, value_heads)
            return (weighted / totals.T[:, :, None]).reshape(FRAMES, HEADS * HEAD_DIM).astype(jnp.bfloat16)
        return lax.map(query_block, query_blocks).reshape(LENGTH, HEADS * HEAD_DIM)
    attended = lax.map(one_record, (query, keys, values))
    projected = jnp.dot(attended.reshape(-1, HEADS * HEAD_DIM), w_out, preferred_element_type=jnp.float32)
    hidden = (resid.astype(jnp.float32) + projected.reshape(RECS, LENGTH, D)).astype(jnp.bfloat16)
    hidden = lax.optimization_barrier(hidden)
    x_normed, inv_norm = layer_stats(hidden.astype(jnp.float32))
    normed = (x_normed * norm_gain).astype(jnp.bfloat16)
    glu_out = jnp.dot(normed.reshape(-1, D), w_in, preferred_element_type=jnp.float32).reshape(RECS, LENGTH, 2 * CH)
    left_half = glu_out[:, :, :CH]
    right_sig = jax.nn.sigmoid(glu_out[:, :, CH:])
    gated = lax.optimization_barrier((left_half * right_sig).astype(jnp.bfloat16))
    rim_width = (TAPS - 1) // 2
    glu_padded = jnp.pad(gated, ((0, 0), (rim_width, rim_width), (0, 0)))
    conv_out = depthwise(glu_padded, kernel, LENGTH)
    conv_act, d_act, z_normed, d_conv = conv_tail(conv_out, cotangent, conv_gain, conv_bias)
    d_conv = lax.optimization_barrier(d_conv)
    grad_padded = jnp.pad(d_conv, ((0, 0), (rim_width, rim_width), (0, 0)))
    d_gated = depthwise(grad_padded, kernel[::-1], LENGTH)
    tap_terms = [lax.optimization_barrier(jnp.sum(d_conv.astype(jnp.float32) * glu_padded[:, tap_index:tap_index + LENGTH].astype(jnp.float32), axis=(0, 1))) for tap_index in range(TAPS)]
    factor = 1.0 / math.sqrt(RECS * LENGTH)
    d_kernel = jnp.stack(tap_terms) * factor
    d_conv_gain = lax.optimization_barrier(jnp.sum(d_act * z_normed, axis=(0, 1))) * factor
    d_conv_bias = lax.optimization_barrier(jnp.sum(d_act, axis=(0, 1))) * factor
    d_glu = jnp.concatenate([d_gated * right_sig, d_gated * left_half * right_sig * (1.0 - right_sig)], axis=2).astype(jnp.bfloat16)
    d_normed = jnp.einsum('rfc,dc->rfd', d_glu.astype(jnp.float32), w_in.astype(jnp.float32))
    d_hidden = norm_back(d_normed * norm_gain, x_normed, inv_norm).astype(jnp.bfloat16)
    return (conv_act, d_hidden, d_kernel, d_conv_gain, d_conv_bias)
```

```python
import functools
import math

import jax
import jax.numpy as jnp
from jax import lax
from jax.experimental import pallas as pl
from jax.experimental.pallas import tpu as pltpu
from jax.sharding import PartitionSpec as P

HEADS = 8
HEAD_DIM = 64
POOL = 4
EPSILON = 1e-05

LANES = 128
HALO = 32
F32 = jnp.float32
BF16 = jnp.bfloat16

VMEM = pl.BlockSpec(memory_space=pltpu.VMEM)


def dot(a, b):
    return lax.dot_general(a, b, (((1,), (0,)), ((), ())), preferred_element_type=F32)


def dot_t(a, b):
    return lax.dot_general(a, b, (((1,), (1,)), ((), ())), preferred_element_type=F32)


def row_mean(x):
    return jnp.sum(x, axis=-1, keepdims=True) * (1.0 / x.shape[-1])


def pack_kernel(
    keys, values, q_head, q_tail, r_head, r_tail, c_head, c_tail, to_left, to_right, own
):
    frames, width = keys.shape
    pooled = frames // POOL
    row = lax.broadcasted_iota(jnp.int32, (pooled, frames), 0)
    col = lax.broadcasted_iota(jnp.int32, (pooled, frames), 1)
    mean = jnp.where(col // POOL == row, 1.0 / POOL, 0.0).astype(BF16)
    for place, source in enumerate((keys, values)):
        block = dot(mean, source[...]).astype(BF16)
        columns = pl.ds(place * width, width)
        own[:, columns] = block
        to_left[0:pooled, columns] = block
        to_right[0:pooled, columns] = block
    model = r_head.shape[1]
    base = 2 * width
    for target, parts in ((to_left, (q_head, r_head, c_head)), (to_right, (q_tail, r_tail, c_tail))):
        at = base
        for part in parts:
            target[0:HALO, pl.ds(at, part.shape[1])] = part[...]
            at += part.shape[1]


def main_kernel(count, blocks, *refs):
    (query, resid, cotangent, w_out, norm_gain, w_in, kernel, conv_gain, conv_bias) = refs[:9]
    (from_left, from_right) = refs[9:11]
    kvs = refs[11 : 11 + blocks]
    (conv_act, x_norm, inv_norm, left_out, sig_out, d_conv, sums) = refs[11 + blocks : 18 + blocks]
    (q_all, kv_all, att, hid, normed, gated, conv, glu, taps) = refs[18 + blocks :]
    frames, width = query.shape
    model = resid.shape[1]
    channels = w_in.shape[1] // 2
    rows = frames + 2 * HALO
    n_taps = kernel.shape[0]
    rim = (n_taps - 1) // 2
    me = lax.axis_index("ctx")
    first = me == 0
    last = me == count - 1
    main = pl.ds(HALO, frames)

    at = 0
    for kv in kvs:
        keep = kv.shape[0]
        kv_all[pl.ds(at, keep), :] = kv[:, 0 : 2 * width]
        at += keep
    keylen = at
    base = 2 * width
    q_all[0:HALO, :] = from_left[0:HALO, base : base + width]
    q_all[main, :] = query[...]
    q_all[HALO + frames :, :] = from_right[0:HALO, base : base + width]

    lane = lax.broadcasted_iota(jnp.int32, (keylen, LANES), 1)
    low = lane < HEAD_DIM
    zero = jnp.zeros((keylen, LANES), BF16)
    ones_low = jnp.where(low, 1.0, 0.0).astype(BF16)
    ones_high = jnp.where(low, 0.0, 1.0).astype(BF16)
    scale = 1.0 / math.sqrt(HEAD_DIM)
    for pair in range(width // LANES):
        cols = pl.ds(pair * LANES, LANES)
        k_pair = kv_all[:, cols]
        v_pair = kv_all[:, pl.ds(width + pair * LANES, LANES)]
        q_pair = q_all[:, cols]
        weighted = None
        for keep_low in (True, False):
            k_head = jnp.where(low, k_pair, zero) if keep_low else jnp.where(low, zero, k_pair)
            v_head = jnp.where(low, v_pair, zero) if keep_low else jnp.where(low, zero, v_pair)
            ones = ones_low if keep_low else ones_high
            scores = dot_t(q_pair, k_head)
            top = jnp.max(scores, axis=-1, keepdims=True)
            probs = jnp.exp((scores - top) * scale).astype(BF16)
            part = dot(probs, jnp.concatenate([v_head, ones], axis=1))
            weighted = part if weighted is None else weighted + part
        att[:, cols] = (weighted[:, :LANES] / weighted[:, LANES:]).astype(BF16)

    step = 256
    for n in range(model // step):
        cols = pl.ds(n * step, step)
        out = dot(att[...], w_out[:, cols])
        at = base + width + n * step
        hid[0:HALO, cols] = (
            (from_left[0:HALO, at : at + step].astype(F32) + out[:HALO]).astype(BF16).astype(F32)
        )
        hid[main, cols] = (
            (resid[:, cols].astype(F32) + out[HALO : HALO + frames]).astype(BF16).astype(F32)
        )
        hid[HALO + frames :, cols] = (
            (from_right[0:HALO, at : at + step].astype(F32) + out[HALO + frames :])
            .astype(BF16)
            .astype(F32)
        )

    gain = norm_gain[...]
    for r in range(0, rows, 32):
        x = hid[r : r + 32, :]
        x = x - row_mean(x)
        inv = lax.rsqrt(row_mean(x * x) + EPSILON)
        x = x * inv
        normed[r : r + 32, :] = (x * gain).astype(BF16)
        if HALO <= r < HALO + frames:
            x_norm[r - HALO : r - HALO + 32, :] = x
            inv_norm[r - HALO : r - HALO + 32, :] = jnp.broadcast_to(inv, (32, LANES))

    for n in range(2 * channels // step):
        cols = pl.ds(n * step, step)
        glu[:, cols] = dot(normed[...], w_in[:, cols])
    for r in range(0, rows, 32):
        left = glu[r : r + 32, 0:channels]
        sig = jax.nn.sigmoid(glu[r : r + 32, channels:])
        out = (left * sig).astype(BF16).astype(F32)
        if r < HALO:
            out = jnp.where(first, 0.0, out)
        elif r >= HALO + frames:
            out = jnp.where(last, 0.0, out)
        else:
            left_out[r - HALO : r - HALO + 32, :] = left
            sig_out[r - HALO : r - HALO + 32, :] = sig
        for c in range(channels // LANES):
            gated[c, r : r + 32, :] = out[:, c * LANES : (c + 1) * LANES]

    edge = HALO // 2
    span = frames + HALO
    for c in range(channels // LANES):
        acc = jnp.zeros((span, LANES), F32)
        for t in range(n_taps):
            tap = kernel[t : t + 1, c * LANES : (c + 1) * LANES]
            acc = acc + tap * gated[c, pl.ds(edge + t - rim, span), :]
        conv[:, c * LANES : (c + 1) * LANES] = acc

    gain = conv_gain[...]
    bias = conv_bias[...]
    at = base + width + model
    sum_gain = jnp.zeros((8, channels), F32)
    sum_bias = jnp.zeros((8, channels), F32)
    for r in range(0, span, 16):
        z = conv[r : r + 16, :]
        z = z - row_mean(z)
        inv = lax.rsqrt(row_mean(z * z) + EPSILON)
        z = z * inv
        act_in = z * gain + bias
        sig = jax.nn.sigmoid(act_in)
        f = r - edge
        if f < 0:
            cot = from_left[edge:HALO, at : at + channels]
        elif f >= frames:
            cot = from_right[0:edge, at : at + channels]
        else:
            cot = cotangent[f : f + 16, :]
        act = act_in * sig
        d_act = cot.astype(F32) * (sig + act * (1.0 - sig))
        if 0 <= f < frames:
            conv_act[f : f + 16, :] = act.astype(BF16)
            d_gain = d_act * z
            sum_gain = sum_gain + d_gain[:8] + d_gain[8:]
            sum_bias = sum_bias + d_act[:8] + d_act[8:]
        g = d_act * gain
        d = (inv * (g - row_mean(g) - z * row_mean(g * z))).astype(BF16).astype(F32)
        if f < 0:
            d = jnp.where(first, 0.0, d)
        elif f >= frames:
            d = jnp.where(last, 0.0, d)
        for c in range(channels // LANES):
            d_conv[c, r : r + 16, :] = d[:, c * LANES : (c + 1) * LANES]
    sums[n_taps : n_taps + 1, :] = jnp.sum(sum_gain, axis=0, keepdims=True)
    sums[n_taps + 1 : n_taps + 2, :] = jnp.sum(sum_bias, axis=0, keepdims=True)

    for c in range(channels // LANES):
        cols = slice(c * LANES, (c + 1) * LANES)
        accs = [jnp.zeros((8, LANES), F32) for _ in range(n_taps)]
        for r in range(0, frames, 8):
            d = d_conv[c, edge + r : edge + r + 8, :]
            for t in range(n_taps):
                accs[t] = accs[t] + d * gated[c, pl.ds(HALO + r + t - rim, 8), :]
        for t in range(n_taps):
            taps[t * 8 : t * 8 + 8, :] = accs[t]
        total = taps[pl.ds(0, n_taps, stride=8), :]
        for s in range(1, 8):
            total = total + taps[pl.ds(s, n_taps, stride=8), :]
        sums[0:n_taps, cols] = total


def back_kernel(
    kernel, norm_gain, w_in, x_norm, inv_norm, left, sig, d_conv, d_hidden, d_glu, d_normed
):
    frames, channels = left.shape
    n_taps = kernel.shape[0]
    rim = (n_taps - 1) // 2
    edge = HALO // 2
    for c in range(channels // LANES):
        cols = slice(c * LANES, (c + 1) * LANES)
        acc = jnp.zeros((frames, LANES), F32)
        for t in range(n_taps):
            acc = acc + kernel[t : t + 1, cols] * d_conv[c, pl.ds(edge - t + rim, frames), :]
        sg = sig[:, cols]
        d_left = acc * sg
        d_glu[:, cols] = d_left.astype(BF16)
        d_glu[:, channels + c * LANES : channels + (c + 1) * LANES] = (
            d_left * left[:, cols] * (1.0 - sg)
        ).astype(BF16)
    model = w_in.shape[0]
    step = 256
    for n in range(model // step):
        d_normed[:, pl.ds(n * step, step)] = dot_t(d_glu[...], w_in[pl.ds(n * step, step), :])
    gain = norm_gain[...]
    for r in range(0, frames, 32):
        g = d_normed[r : r + 32, :] * gain
        x = x_norm[r : r + 32, :]
        inv = inv_norm[r : r + 32, 0:1]
        out = inv * (g - row_mean(g) - x * row_mean(g * x))
        d_hidden[r : r + 32, :] = out.astype(BF16)


def exchange(axis, count, own, to_left, to_right):
    if count == 4:
        from_left = lax.ppermute(to_right, axis, [(i, (i + 1) % 4) for i in range(4)])
        from_right = lax.ppermute(to_left, axis, [((i + 1) % 4, i) for i in range(4)])
        far = lax.ppermute(own, axis, [(i, (i + 2) % 4) for i in range(4)])
        return from_left, from_right, (own, from_left, from_right, far)
    every = lax.all_gather(own, axis, axis=0, tiled=True)
    from_left = lax.ppermute(to_right, axis, [(i, (i + 1) % count) for i in range(count)])
    from_right = lax.ppermute(to_left, axis, [((i + 1) % count, i) for i in range(count)])
    return from_left, from_right, (every,)


def total_of(sums, ctx, dp):
    if ctx == 4 and dp == 4:
        flip = lambda k: [(i, i ^ k) for i in range(4)]
        sums = sums + lax.ppermute(sums, "dp", flip(1))
        sums = sums.astype(BF16)
        sums = (sums.astype(F32) + lax.ppermute(sums, "dp", flip(2)).astype(F32)).astype(BF16)
        one, two, three = (lax.ppermute(sums, "ctx", flip(k)) for k in (1, 2, 3))
        return (sums.astype(F32) + one.astype(F32)) + (two.astype(F32) + three.astype(F32))
    return lax.psum(sums, ("ctx", "dp"))


def per_device(
    resid, query, keys, values, w_out, norm_gain, w_in, kernel, conv_gain, conv_bias, cotangent
):
    frames, model = resid.shape[1:]
    width = query.shape[2]
    channels = cotangent.shape[2]
    n_taps = kernel.shape[0]
    ctx, dp = lax.axis_size("ctx"), lax.axis_size("dp")
    resid, query, keys, values, cotangent = (
        x.reshape(x.shape[1:]) for x in (resid, query, keys, values, cotangent)
    )
    norm_gain, conv_gain, conv_bias = (x.reshape(1, -1) for x in (norm_gain, conv_gain, conv_bias))
    pooled = frames // POOL
    message = 2 * width + width + model + channels
    assert pooled <= HALO

    def head(n):
        return pl.BlockSpec((HALO, n), lambda i: (0, 0))

    def tail(n):
        return pl.BlockSpec((HALO, n), lambda i: (frames // HALO - 1, 0))

    to_left, to_right, own = pl.pallas_call(
        pack_kernel,
        out_shape=(
            jax.ShapeDtypeStruct((HALO, message), BF16),
            jax.ShapeDtypeStruct((HALO, message), BF16),
            jax.ShapeDtypeStruct((pooled, 2 * width), BF16),
        ),
        grid=(1,),
        in_specs=[VMEM, VMEM]
        + [spec(n) for n in (width, model, channels) for spec in (head, tail)],
        out_specs=(VMEM,) * 3,
    )(keys, values, query, query, resid, resid, cotangent, cotangent)

    from_left, from_right, kvs = exchange("ctx", ctx, own, to_left, to_right)

    rows = frames + 2 * HALO
    span = frames + HALO
    shape = jax.ShapeDtypeStruct
    conv_act, x_norm, inv_norm, left, sig, d_conv, sums = pl.pallas_call(
        functools.partial(main_kernel, ctx, len(kvs)),
        out_shape=(
            shape((frames, channels), BF16),
            shape((frames, model), F32),
            shape((frames, LANES), F32),
            shape((frames, channels), F32),
            shape((frames, channels), F32),
            shape((channels // LANES, span, LANES), F32),
            shape((n_taps + 2, channels), F32),
        ),
        in_specs=[VMEM] * (11 + len(kvs)),
        out_specs=(VMEM,) * 7,
        scratch_shapes=[
            pltpu.VMEM((rows, width), BF16),
            pltpu.VMEM((pooled * ctx, 2 * width), BF16),
            pltpu.VMEM((rows, width), BF16),
            pltpu.VMEM((rows, model), F32),
            pltpu.VMEM((rows, model), BF16),
            pltpu.VMEM((channels // LANES, rows, LANES), F32),
            pltpu.VMEM((span, channels), F32),
            pltpu.VMEM((rows, 2 * channels), F32),
            pltpu.VMEM((n_taps * 8, LANES), F32),
        ],
        compiler_params=pltpu.CompilerParams(vmem_limit_bytes=40 * 2**20),
    )(
        query,
        resid,
        cotangent,
        w_out,
        norm_gain,
        w_in,
        kernel,
        conv_gain,
        conv_bias,
        from_left,
        from_right,
        *kvs,
    )

    d_hidden = pl.pallas_call(
        back_kernel,
        out_shape=shape((frames, model), BF16),
        in_specs=[VMEM] * 8,
        out_specs=VMEM,
        scratch_shapes=[
            pltpu.VMEM((frames, 2 * channels), BF16),
            pltpu.VMEM((frames, model), F32),
        ],
        compiler_params=pltpu.CompilerParams(vmem_limit_bytes=24 * 2**20),
    )(kernel, norm_gain, w_in, x_norm, inv_norm, left, sig, d_conv)

    factor = 1.0 / math.sqrt(frames * ctx * dp)
    total = total_of(sums, ctx, dp) * factor
    return (conv_act[None], d_hidden[None], total[:n_taps], total[n_taps], total[n_taps + 1])


def solution(mesh):
    split = P(("groups", "dp"), "ctx", None)
    return jax.shard_map(
        per_device,
        mesh=mesh,
        in_specs=(split,) * 4 + (P(),) * 6 + (split,),
        out_specs=(split, split, P("groups", None), P("groups"), P("groups")),
        check_vma=False,
    )
```

```python
import functools
import math

import jax
import jax.numpy as jnp
from jax import lax
from jax.experimental import pallas as pl
from jax.experimental.pallas import tpu as pltpu
from jax.sharding import PartitionSpec as P

HEAD_DIM = 64
POOL = 4
EPSILON = 1e-05

LANES = 128
HALO = 16
F32 = jnp.float32
BF16 = jnp.bfloat16

VMEM = pl.BlockSpec(memory_space=pltpu.VMEM)
HBM = pl.BlockSpec(memory_space=pltpu.HBM)
shape = jax.ShapeDtypeStruct


def dot(a, b):
    return lax.dot_general(a, b, (((1,), (0,)), ((), ())), preferred_element_type=F32)


def dot_t(a, b):
    return lax.dot_general(a, b, (((1,), (1,)), ((), ())), preferred_element_type=F32)


def row_mean(x):
    return jnp.sum(x, axis=-1, keepdims=True) * (1.0 / x.shape[-1])


def in_hbm(*arrays):
    return [pltpu.with_memory_space_constraint(x, pltpu.HBM) for x in arrays]


def swapped(pairwise):
    return lax.rem(lax.axis_index("ctx"), 2) == 1 if pairwise else False


def pack_kernel(pairwise, keys, values, query, resid, own, to_a, to_b, kv, sem, kv_sem):
    frames, width = keys.shape
    model = resid.shape[1]
    pooled = frames // POOL
    swap = swapped(pairwise)
    loads = [
        pltpu.make_async_copy(source, kv.at[place], kv_sem.at[place])
        for place, source in enumerate((keys, values))
    ]
    for load in loads:
        load.start()
    edges = []
    for target, near in ((to_a, True), (to_b, False)):
        start = jnp.where(swap, 0 if near else frames - HALO, frames - HALO if near else 0)
        start = pl.multiple_of(start.astype(jnp.int32), HALO)
        at = 2 * pooled
        for source, column in [(query, 0)] + [(resid, c) for c in range(0, model, width)]:
            edges.append(
                pltpu.make_async_copy(
                    source.at[pl.ds(start, HALO), pl.ds(column, width)],
                    target.at[pl.ds(at, HALO), :],
                    sem.at[len(edges)],
                )
            )
            edges[-1].start()
            at += HALO
    row = lax.broadcasted_iota(jnp.int32, (pooled, frames), 0)
    col = lax.broadcasted_iota(jnp.int32, (pooled, frames), 1)
    mean = jnp.where(col // POOL == row, 1.0 / POOL, 0.0).astype(BF16)
    for place, load in enumerate(loads):
        load.wait()
        block = dot(mean, kv[place]).astype(BF16)
        rows = pl.ds(place * pooled, pooled)
        own[rows, :] = block
        to_a[rows, :] = block
        to_b[rows, :] = block
    for edge in edges:
        edge.wait()


def fetch_kernel(count, after, *refs):
    sources, targets, sem = refs[:count], refs[count : 2 * count], refs[2 * count]
    copies = [
        pltpu.make_async_copy(a, b, sem.at[i]) for i, (a, b) in enumerate(zip(sources, targets))
    ]
    for copy in copies:
        copy.start()
    for copy in copies:
        copy.wait()


def main_kernel(pairwise, count, kv_places, *refs):
    (query, resid, cotangent, w_out, norm_gain, w_in, kernel, conv_gain, conv_bias) = refs[:9]
    from_a, from_b = refs[9:11]
    n_kv = len(kv_places)
    kvs = refs[11 : 11 + n_kv]
    (conv_act, x_norm, inv_norm, left_out, sig_out, d_conv) = refs[11 + n_kv : 17 + n_kv]
    to_a, to_b, sums = refs[17 + n_kv : 20 + n_kv]
    (q_all, r_edge, k_all, v_all, att, hid, normed, gated, conv, glu, taps, act_out, pack, sem) = (
        refs[20 + n_kv :]
    )
    frames, width = query.shape
    model = resid.shape[1]
    channels = w_in.shape[1] // 2
    rows = frames + 2 * HALO
    n_taps = kernel.shape[0]
    rim = (n_taps - 1) // 2
    pooled = frames // POOL
    me = lax.axis_index("ctx")
    first = me == 0
    last = me == count - 1
    swap = swapped(pairwise)
    main = pl.ds(HALO, frames)

    at = 0
    for ref, (k_row, v_row, keep) in zip(kvs, kv_places):
        if k_row is not None:
            k_all[pl.ds(at, keep), :] = ref[pl.ds(k_row, keep), :]
        if v_row is not None:
            v_all[pl.ds(at, keep), :] = ref[pl.ds(v_row, keep), :]
            at += keep
    keylen = at
    q_all[main, :] = query[...]
    base = 2 * pooled
    for left_side in (True, False):
        edge_rows = pl.ds(0 if left_side else HALO + frames, HALO)
        r_rows = pl.ds(0 if left_side else HALO, HALO)
        near, other = (from_b, from_a) if left_side else (from_a, from_b)

        def pick(start):
            rows_in = pl.ds(start, HALO)
            return jnp.where(swap, other[rows_in, :], near[rows_in, :])

        q_all[edge_rows, :] = pick(base)
        for piece in range(model // width):
            r_edge[r_rows, pl.ds(piece * width, width)] = pick(base + HALO * (1 + piece))

    lane = lax.broadcasted_iota(jnp.int32, (keylen, LANES), 1)
    low = lane < HEAD_DIM
    zero = jnp.zeros((keylen, LANES), BF16)
    ones_low = jnp.where(low, 1.0, 0.0).astype(BF16)
    ones_high = jnp.where(low, 0.0, 1.0).astype(BF16)
    scale = 1.0 / math.sqrt(HEAD_DIM)
    for pair in range(width // LANES):
        cols = pl.ds(pair * LANES, LANES)
        k_pair = k_all[:, cols]
        v_pair = v_all[:, cols]
        q_pair = q_all[:, cols]
        weighted = None
        for keep_low in (True, False):
            k_head = jnp.where(low, k_pair, zero) if keep_low else jnp.where(low, zero, k_pair)
            v_head = jnp.where(low, v_pair, zero) if keep_low else jnp.where(low, zero, v_pair)
            ones = ones_low if keep_low else ones_high
            scores = dot_t(q_pair, k_head)
            top = jnp.max(scores, axis=-1, keepdims=True)
            probs = jnp.exp((scores - top) * scale).astype(BF16)
            part = dot(probs, jnp.concatenate([v_head, ones], axis=1))
            weighted = part if weighted is None else weighted + part
        att[:, cols] = (weighted[:, :LANES] / weighted[:, LANES:]).astype(BF16)

    step = 256
    for n in range(model // step):
        cols = pl.ds(n * step, step)
        out = dot(att[...], w_out[:, cols])
        for rows_in, res in (
            (slice(0, HALO), r_edge[0:HALO, cols]),
            (slice(HALO, HALO + frames), resid[:, cols]),
            (slice(HALO + frames, rows), r_edge[HALO:, cols]),
        ):
            hid[rows_in, cols] = (res.astype(F32) + out[rows_in]).astype(BF16).astype(F32)

    gain = norm_gain[...]
    for r in range(0, rows, 32):
        x = hid[r : r + 32, :]
        x = x - row_mean(x)
        inv = lax.rsqrt(row_mean(x * x) + EPSILON)
        x = x * inv
        normed[r : r + 32, :] = (x * gain).astype(BF16)
        x_norm[r : r + 32, :] = x
        inv_norm[r : r + 32, :] = jnp.broadcast_to(inv, (32, LANES))

    for n in range(2 * channels // step):
        cols = pl.ds(n * step, step)
        glu[:, cols] = dot(normed[...], w_in[:, cols])
    for r in range(0, rows, 16):
        left = glu[r : r + 16, 0:channels]
        sig = jax.nn.sigmoid(glu[r : r + 16, channels:])
        out = (left * sig).astype(BF16).astype(F32)
        if r < HALO:
            out = jnp.where(first, 0.0, out)
        elif r >= HALO + frames:
            out = jnp.where(last, 0.0, out)
        else:
            left_out[r - HALO : r - HALO + 16, :] = left
            sig_out[r - HALO : r - HALO + 16, :] = sig
        for c in range(channels // LANES):
            gated[c, r : r + 16, :] = out[:, c * LANES : (c + 1) * LANES]

    for c in range(channels // LANES):
        cols = slice(c * LANES, (c + 1) * LANES)
        acc = jnp.zeros((frames, LANES), F32)
        for t in range(n_taps):
            acc = acc + kernel[t : t + 1, cols] * gated[c, pl.ds(HALO + t - rim, frames), :]
        conv[:, cols] = acc

    gain = conv_gain[...]
    bias = conv_bias[...]
    sum_gain = jnp.zeros((8, channels), F32)
    sum_bias = jnp.zeros((8, channels), F32)
    for r in range(0, frames, 16):
        z = conv[r : r + 16, :]
        z = z - row_mean(z)
        inv = lax.rsqrt(row_mean(z * z) + EPSILON)
        z = z * inv
        act_in = z * gain + bias
        sig = jax.nn.sigmoid(act_in)
        act = act_in * sig
        act_out[r : r + 16, :] = act.astype(BF16)
        d_act = cotangent[r : r + 16, :].astype(F32) * (sig + act * (1.0 - sig))
        d_gain = d_act * z
        sum_gain = sum_gain + d_gain[:8] + d_gain[8:]
        sum_bias = sum_bias + d_act[:8] + d_act[8:]
        g = d_act * gain
        d = (inv * (g - row_mean(g) - z * row_mean(g * z))).astype(BF16).astype(F32)
        for c in range(channels // LANES):
            d_conv[c, r : r + 16, :] = d[:, c * LANES : (c + 1) * LANES]
    write = pltpu.make_async_copy(act_out, conv_act, sem)
    write.start()
    pack[n_taps : n_taps + 1, :] = jnp.sum(sum_gain, axis=0, keepdims=True)
    pack[n_taps + 1 : n_taps + 2, :] = jnp.sum(sum_bias, axis=0, keepdims=True)

    for c in range(channels // LANES):
        cols = slice(c * LANES, (c + 1) * LANES)
        accs = [jnp.zeros((8, LANES), F32) for _ in range(n_taps)]
        for r in range(0, frames, 8):
            d = d_conv[c, r : r + 8, :]
            for t in range(n_taps):
                accs[t] = accs[t] + d * gated[c, pl.ds(HALO + r + t - rim, 8), :]
        for t in range(n_taps):
            taps[t * 8 : t * 8 + 8, :] = accs[t]
        total = taps[pl.ds(0, n_taps, stride=8), :]
        for s in range(1, 8):
            total = total + taps[pl.ds(s, n_taps, stride=8), :]
        pack[0:n_taps, cols] = total

    used = n_taps + 2
    if pairwise:
        sums[...] = pack[0:used, :].astype(BF16)
    else:
        sums[...] = pack[0:used, :]
    for target, near in ((to_a, True), (to_b, False)):
        for c in range(channels // LANES):
            tail, head = d_conv[c, frames - rim :, :], d_conv[c, 0:rim, :]
            edge = jnp.where(swap, head, tail) if near else jnp.where(swap, tail, head)
            pack[used : used + rim, c * LANES : (c + 1) * LANES] = edge
        target[...] = pack[...].astype(BF16)
    write.wait()


def back_kernel(
    pairwise, count, kernel, norm_gain, w_in, x_norm, inv_norm, left, sig, d_conv, from_a, from_b,
    d_hidden, padded, edges, d_glu, d_normed,
):
    frames, channels = left.shape
    n_taps = kernel.shape[0]
    rim = (n_taps - 1) // 2
    me = lax.axis_index("ctx")
    swap = swapped(pairwise)
    used = n_taps + 2
    edges[0] = from_a[...].astype(F32)
    edges[1] = from_b[...].astype(F32)
    for c in range(channels // LANES):
        cols = slice(c * LANES, (c + 1) * LANES)
        a, b = edges[0, used : used + rim, cols], edges[1, used : used + rim, cols]
        on_left = jnp.where(me == 0, 0.0, jnp.where(swap, a, b))
        on_right = jnp.where(me == count - 1, 0.0, jnp.where(swap, b, a))
        padded[HALO - rim : HALO, cols] = on_left
        padded[HALO : HALO + frames, cols] = d_conv[c]
        padded[HALO + frames : HALO + frames + rim, cols] = on_right
        acc = jnp.zeros((frames, LANES), F32)
        for t in range(n_taps):
            acc = acc + kernel[t : t + 1, cols] * padded[pl.ds(HALO - t + rim, frames), cols]
        sg = sig[:, cols]
        d_left = acc * sg
        d_glu[:, cols] = d_left.astype(BF16)
        d_glu[:, channels + c * LANES : channels + (c + 1) * LANES] = (
            d_left * left[:, cols] * (1.0 - sg)
        ).astype(BF16)
    model = w_in.shape[0]
    step = 256
    for n in range(model // step):
        d_normed[:, pl.ds(n * step, step)] = dot_t(d_glu[...], w_in[pl.ds(n * step, step), :])
    gain = norm_gain[...]
    for r in range(0, frames, 32):
        g = d_normed[r : r + 32, :] * gain
        x = x_norm[HALO + r : HALO + r + 32, :]
        inv = inv_norm[HALO + r : HALO + r + 32, 0:1]
        out = inv * (g - row_mean(g) - x * row_mean(g * x))
        d_hidden[r : r + 32, :] = out.astype(BF16)


def total_kernel(factor, one, two, three, four, d_kernel, d_gain, d_bias):
    n_taps = d_kernel.shape[0]
    total = (one[...].astype(F32) + two[...].astype(F32)) + (
        three[...].astype(F32) + four[...].astype(F32)
    )
    total = total * factor
    d_kernel[...] = total[0:n_taps]
    d_gain[...] = total[n_taps : n_taps + 1]
    d_bias[...] = total[n_taps + 1 :]


def flips(array, axis, which):
    return [lax.ppermute(array, axis, [(i, i ^ k) for i in range(4)]) for k in which]


def to_neighbours(pairwise, count, to_a, to_b):
    if pairwise:
        return flips(to_a, "ctx", (1,)) + flips(to_b, "ctx", (3,))
    return [
        lax.ppermute(to_b, "ctx", [((i + 1) % count, i) for i in range(count)]),
        lax.ppermute(to_a, "ctx", [(i, (i + 1) % count) for i in range(count)]),
    ]


def per_device(
    resid, query, keys, values, w_out, norm_gain, w_in, kernel, conv_gain, conv_bias, cotangent
):
    frames, model = resid.shape[1:]
    width = query.shape[2]
    channels = cotangent.shape[2]
    n_taps = kernel.shape[0]
    rim = (n_taps - 1) // 2
    ctx, dp = lax.axis_size("ctx"), lax.axis_size("dp")
    pairwise = ctx == 4 and dp == 4
    resid, query, keys, values, cotangent = (
        x.reshape(x.shape[1:]) for x in (resid, query, keys, values, cotangent)
    )
    norm_gain, conv_gain, conv_bias = (x.reshape(1, -1) for x in (norm_gain, conv_gain, conv_bias))
    pooled = frames // POOL
    message = 2 * pooled + HALO * (1 + model // width)
    n_edges = 2 * (1 + model // width)

    own, to_a, to_b = pl.pallas_call(
        functools.partial(pack_kernel, pairwise),
        out_shape=(
            shape((2 * pooled, width), BF16),
            shape((message, width), BF16),
            shape((message, width), BF16),
        ),
        in_specs=[HBM] * 4,
        out_specs=(VMEM,) * 3,
        scratch_shapes=[
            pltpu.VMEM((2, frames, width), BF16),
            pltpu.SemaphoreType.DMA((n_edges,)),
            pltpu.SemaphoreType.DMA((2,)),
        ],
        compiler_params=pltpu.CompilerParams(vmem_limit_bytes=4 * 2**20),
    )(*in_hbm(keys, values, query, resid))

    from_a, from_b = to_neighbours(pairwise, ctx, to_a, to_b)
    if pairwise:
        (far,) = flips(own, "ctx", (2,))
        kvs = (own, from_a, from_b, far)
        kv_places = ((0, pooled, pooled),) * 4
    else:
        kvs = tuple(
            lax.all_gather(part, "ctx", axis=0, tiled=True) for part in (own[:pooled], own[pooled:])
        )
        kv_places = ((0, None, pooled * ctx), (None, 0, pooled * ctx))

    operands = (
        query, resid, cotangent, w_out, norm_gain, w_in, kernel, conv_gain, conv_bias,
    )
    operands = pl.pallas_call(
        functools.partial(fetch_kernel, len(operands)),
        out_shape=tuple(shape(x.shape, x.dtype) for x in operands),
        in_specs=[HBM] * (1 + len(operands)),
        out_specs=(VMEM,) * len(operands),
        scratch_shapes=[pltpu.SemaphoreType.DMA((len(operands),))],
        compiler_params=pltpu.CompilerParams(vmem_limit_bytes=8 * 2**20),
    )(own, *in_hbm(*operands))
    norm_gain, w_in, kernel = operands[4:7]

    rows = frames + 2 * HALO
    used = n_taps + 2
    conv_act, x_norm, inv_norm, left, sig, d_conv, to_a, to_b, sums = pl.pallas_call(
        functools.partial(main_kernel, pairwise, ctx, kv_places),
        out_shape=(
            shape((frames, channels), BF16),
            shape((rows, model), F32),
            shape((rows, LANES), F32),
            shape((frames, channels), F32),
            shape((frames, channels), F32),
            shape((channels // LANES, frames, LANES), F32),
            shape((used + rim, channels), BF16),
            shape((used + rim, channels), BF16),
            shape((used, channels), BF16 if pairwise else F32),
        ),
        in_specs=[VMEM] * (11 + len(kvs)),
        out_specs=(HBM,) + (VMEM,) * 8,
        scratch_shapes=[
            pltpu.VMEM((rows, width), BF16),
            pltpu.VMEM((2 * HALO, model), BF16),
            pltpu.VMEM((pooled * ctx, width), BF16),
            pltpu.VMEM((pooled * ctx, width), BF16),
            pltpu.VMEM((rows, width), BF16),
            pltpu.VMEM((rows, model), F32),
            pltpu.VMEM((rows, model), BF16),
            pltpu.VMEM((channels // LANES, rows, LANES), F32),
            pltpu.VMEM((frames, channels), F32),
            pltpu.VMEM((rows, 2 * channels), F32),
            pltpu.VMEM((n_taps * 8, LANES), F32),
            pltpu.VMEM((frames, channels), BF16),
            pltpu.VMEM((used + rim, channels), F32),
            pltpu.SemaphoreType.DMA,
        ],
        compiler_params=pltpu.CompilerParams(vmem_limit_bytes=32 * 2**20),
    )(*operands, from_a, from_b, *kvs)

    from_a, from_b = to_neighbours(pairwise, ctx, to_a, to_b)
    if pairwise:
        (far,) = flips(sums, "ctx", (2,))
        near, across = (x[:used].astype(F32) for x in (from_a, from_b))
        sums = ((sums.astype(F32) + near) + (far.astype(F32) + across)).astype(BF16)
        parts = [sums] + flips(sums, "dp", (1, 2, 3))

    d_hidden = pl.pallas_call(
        functools.partial(back_kernel, pairwise, ctx),
        out_shape=shape((frames, model), BF16),
        in_specs=[VMEM] * 10,
        out_specs=VMEM,
        scratch_shapes=[
            pltpu.VMEM((rows, channels), F32),
            pltpu.VMEM((2, used + rim, channels), F32),
            pltpu.VMEM((frames, 2 * channels), BF16),
            pltpu.VMEM((frames, model), F32),
        ],
        compiler_params=pltpu.CompilerParams(vmem_limit_bytes=24 * 2**20),
    )(kernel, norm_gain, w_in, x_norm, inv_norm, left, sig, d_conv, from_a, from_b)

    factor = 1.0 / math.sqrt(frames * ctx * dp)
    if pairwise:
        d_kernel, d_gain, d_bias = pl.pallas_call(
            functools.partial(total_kernel, factor),
            out_shape=(shape((n_taps, channels), F32),) + (shape((1, channels), F32),) * 2,
            in_specs=[VMEM] * 4,
            out_specs=(VMEM,) * 3,
            compiler_params=pltpu.CompilerParams(vmem_limit_bytes=2 * 2**20),
        )(*parts)
        d_gain, d_bias = d_gain.reshape(-1), d_bias.reshape(-1)
    else:
        total = lax.psum(sums, ("ctx", "dp")) * factor
        d_kernel, d_gain, d_bias = total[:n_taps], total[n_taps], total[n_taps + 1]
    return (conv_act[None], d_hidden[None], d_kernel, d_gain, d_bias)


def solution(mesh):
    split = P(("groups", "dp"), "ctx", None)
    return jax.shard_map(
        per_device,
        mesh=mesh,
        in_specs=(split,) * 4 + (P(),) * 6 + (split,),
        out_specs=(split, split, P("groups", None), P("groups"), P("groups")),
        check_vma=False,
    )
```

```python
import functools
import math

import jax
import jax.numpy as jnp
from jax import lax
from jax.experimental import pallas as pl
from jax.experimental.pallas import tpu as pltpu
from jax.sharding import PartitionSpec as P

HEAD_DIM = 64
POOL = 4
EPSILON = 1e-05

LANES = 128
HALO = 16
F32 = jnp.float32
BF16 = jnp.bfloat16

VMEM = pl.BlockSpec(memory_space=pltpu.VMEM)
HBM = pl.BlockSpec(memory_space=pltpu.HBM)
shape = jax.ShapeDtypeStruct


def dot(a, b):
    return lax.dot_general(a, b, (((1,), (0,)), ((), ())), preferred_element_type=F32)


def dot_t(a, b):
    return lax.dot_general(a, b, (((1,), (1,)), ((), ())), preferred_element_type=F32)


def row_mean(x):
    return jnp.sum(x, axis=-1, keepdims=True) * (1.0 / x.shape[-1])


def in_hbm(*arrays):
    return [pltpu.with_memory_space_constraint(x, pltpu.HBM) for x in arrays]


def swapped(pairwise):
    return lax.rem(lax.axis_index("ctx"), 2) == 1 if pairwise else False


def pack_kernel(pairwise, keys, values, query, resid, own, to_a, to_b, kv, sem, kv_sem):
    frames, width = keys.shape
    model = resid.shape[1]
    pooled = frames // POOL
    swap = swapped(pairwise)
    loads = [
        pltpu.make_async_copy(source, kv.at[place], kv_sem.at[place])
        for place, source in enumerate((keys, values))
    ]
    for load in loads:
        load.start()
    edges = []
    for target, near in ((to_a, True), (to_b, False)):
        at = 0
        start = jnp.where(swap, 0 if near else frames - HALO, frames - HALO if near else 0)
        start = pl.multiple_of(start.astype(jnp.int32), HALO)
        for source, column in [(query, 0)] + [(resid, c) for c in range(0, model, width)]:
            edges.append(
                pltpu.make_async_copy(
                    source.at[pl.ds(start, HALO), pl.ds(column, width)],
                    target.at[pl.ds(at, HALO), :],
                    sem.at[len(edges)],
                )
            )
            edges[-1].start()
            at += HALO
    row = lax.broadcasted_iota(jnp.int32, (pooled, frames), 0)
    col = lax.broadcasted_iota(jnp.int32, (pooled, frames), 1)
    mean = jnp.where(col // POOL == row, 1.0 / POOL, 0.0).astype(BF16)
    for place, load in enumerate(loads):
        load.wait()
        block = dot(mean, kv[place]).astype(BF16)
        rows = pl.ds(place * pooled, pooled)
        own[rows, :] = block
    for edge in edges:
        edge.wait()


def fetch_kernel(count, after, *refs):
    sources, targets, sem = refs[:count], refs[count : 2 * count], refs[2 * count]
    copies = [
        pltpu.make_async_copy(a, b, sem.at[i]) for i, (a, b) in enumerate(zip(sources, targets))
    ]
    for copy in copies:
        copy.start()
    for copy in copies:
        copy.wait()


def main_kernel(pairwise, count, kv_places, *refs):
    (query, resid, cotangent, w_out, norm_gain, w_in, kernel, conv_gain, conv_bias) = refs[:9]
    n_kv = len(kv_places)
    kvs = refs[9 : 9 + n_kv]
    from_b, from_a = refs[9 + n_kv : 11 + n_kv]
    (conv_act, x_norm, inv_norm, left_out, sig_out, d_conv) = refs[11 + n_kv : 17 + n_kv]
    to_a, to_b, sums = refs[17 + n_kv : 20 + n_kv]
    (q_all, r_edge, k_all, v_all, att, hid, normed, gated, conv, glu, taps, act_out, pack, sem) = (
        refs[20 + n_kv :]
    )
    frames, width = query.shape
    model = resid.shape[1]
    channels = w_in.shape[1] // 2
    rows = frames + 2 * HALO
    n_taps = kernel.shape[0]
    rim = (n_taps - 1) // 2
    me = lax.axis_index("ctx")
    first = me == 0
    last = me == count - 1
    swap = swapped(pairwise)
    main = pl.ds(HALO, frames)

    at = 0
    for ref, (k_row, v_row, keep) in zip(kvs, kv_places):
        if k_row is not None:
            k_all[pl.ds(at, keep), :] = ref[pl.ds(k_row, keep), :]
        if v_row is not None:
            v_all[pl.ds(at, keep), :] = ref[pl.ds(v_row, keep), :]
            at += keep
    keylen = at
    q_all[main, :] = query[...]
    for left_side in (True, False):
        edge_rows = pl.ds(0 if left_side else HALO + frames, HALO)
        r_rows = pl.ds(0 if left_side else HALO, HALO)

        def pick(start):
            a = from_a[pl.ds(start, HALO), :]
            b = from_b[pl.ds(start, HALO), :]
            return jnp.where(swap, a, b) if left_side else jnp.where(swap, b, a)

        q_all[edge_rows, :] = pick(0)
        for piece in range(model // width):
            r_edge[r_rows, pl.ds(piece * width, width)] = pick(HALO * (1 + piece))

    lane = lax.broadcasted_iota(jnp.int32, (keylen, LANES), 1)
    low = lane < HEAD_DIM
    zero = jnp.zeros((keylen, LANES), BF16)
    ones_low = jnp.where(low, 1.0, 0.0).astype(BF16)
    ones_high = jnp.where(low, 0.0, 1.0).astype(BF16)
    scale = 1.0 / math.sqrt(HEAD_DIM)
    for pair in range(width // LANES):
        cols = pl.ds(pair * LANES, LANES)
        k_pair = k_all[:, cols]
        v_pair = v_all[:, cols]
        q_pair = q_all[:, cols]
        weighted = None
        for keep_low in (True, False):
            k_head = jnp.where(low, k_pair, zero) if keep_low else jnp.where(low, zero, k_pair)
            v_head = jnp.where(low, v_pair, zero) if keep_low else jnp.where(low, zero, v_pair)
            ones = ones_low if keep_low else ones_high
            scores = dot_t(q_pair, k_head)
            top = jnp.max(scores, axis=-1, keepdims=True)
            probs = jnp.exp((scores - top) * scale).astype(BF16)
            part = dot(probs, jnp.concatenate([v_head, ones], axis=1))
            weighted = part if weighted is None else weighted + part
        att[:, cols] = (weighted[:, :LANES] / weighted[:, LANES:]).astype(BF16)

    step = 256
    for n in range(model // step):
        cols = pl.ds(n * step, step)
        out = dot(att[...], w_out[:, cols])
        for rows_in, res in (
            (slice(0, HALO), r_edge[0:HALO, cols]),
            (slice(HALO, HALO + frames), resid[:, cols]),
            (slice(HALO + frames, rows), r_edge[HALO:, cols]),
        ):
            hid[rows_in, cols] = (res.astype(F32) + out[rows_in]).astype(BF16).astype(F32)

    gain = norm_gain[...]
    for r in range(0, rows, 32):
        x = hid[r : r + 32, :]
        x = x - row_mean(x)
        inv = lax.rsqrt(row_mean(x * x) + EPSILON)
        x = x * inv
        normed[r : r + 32, :] = (x * gain).astype(BF16)
        x_norm[r : r + 32, :] = x
        inv_norm[r : r + 32, :] = jnp.broadcast_to(inv, (32, LANES))

    for n in range(2 * channels // step):
        cols = pl.ds(n * step, step)
        glu[:, cols] = dot(normed[...], w_in[:, cols])
    for r in range(0, rows, 16):
        left = glu[r : r + 16, 0:channels]
        sig = jax.nn.sigmoid(glu[r : r + 16, channels:])
        out = (left * sig).astype(BF16).astype(F32)
        if r < HALO:
            out = jnp.where(first, 0.0, out)
        elif r >= HALO + frames:
            out = jnp.where(last, 0.0, out)
        else:
            left_out[r - HALO : r - HALO + 16, :] = left
            sig_out[r - HALO : r - HALO + 16, :] = sig
        for c in range(channels // LANES):
            gated[c, r : r + 16, :] = out[:, c * LANES : (c + 1) * LANES]

    for c in range(channels // LANES):
        cols = slice(c * LANES, (c + 1) * LANES)
        acc = jnp.zeros((frames, LANES), F32)
        for t in range(n_taps):
            acc = acc + kernel[t : t + 1, cols] * gated[c, pl.ds(HALO + t - rim, frames), :]
        conv[:, cols] = acc

    gain = conv_gain[...]
    bias = conv_bias[...]
    sum_gain = jnp.zeros((8, channels), F32)
    sum_bias = jnp.zeros((8, channels), F32)
    for r in range(0, frames, 16):
        z = conv[r : r + 16, :]
        z = z - row_mean(z)
        inv = lax.rsqrt(row_mean(z * z) + EPSILON)
        z = z * inv
        act_in = z * gain + bias
        sig = jax.nn.sigmoid(act_in)
        act = act_in * sig
        act_out[r : r + 16, :] = act.astype(BF16)
        d_act = cotangent[r : r + 16, :].astype(F32) * (sig + act * (1.0 - sig))
        d_gain = d_act * z
        sum_gain = sum_gain + d_gain[:8] + d_gain[8:]
        sum_bias = sum_bias + d_act[:8] + d_act[8:]
        g = d_act * gain
        d = (inv * (g - row_mean(g) - z * row_mean(g * z))).astype(BF16).astype(F32)
        for c in range(channels // LANES):
            d_conv[c, r : r + 16, :] = d[:, c * LANES : (c + 1) * LANES]
    write = pltpu.make_async_copy(act_out, conv_act, sem)
    write.start()
    pack[n_taps : n_taps + 1, :] = jnp.sum(sum_gain, axis=0, keepdims=True)
    pack[n_taps + 1 : n_taps + 2, :] = jnp.sum(sum_bias, axis=0, keepdims=True)

    for c in range(channels // LANES):
        cols = slice(c * LANES, (c + 1) * LANES)
        accs = [jnp.zeros((8, LANES), F32) for _ in range(n_taps)]
        for r in range(0, frames, 8):
            d = d_conv[c, r : r + 8, :]
            for t in range(n_taps):
                accs[t] = accs[t] + d * gated[c, pl.ds(HALO + r + t - rim, 8), :]
        for t in range(n_taps):
            taps[t * 8 : t * 8 + 8, :] = accs[t]
        total = taps[pl.ds(0, n_taps, stride=8), :]
        for s in range(1, 8):
            total = total + taps[pl.ds(s, n_taps, stride=8), :]
        pack[0:n_taps, cols] = total

    used = n_taps + 2
    if pairwise:
        sums[...] = pack[0:used, :].astype(BF16)
    else:
        sums[...] = pack[0:used, :]
    for target, near in ((to_a, True), (to_b, False)):
        for c in range(channels // LANES):
            tail, head = d_conv[c, frames - rim :, :], d_conv[c, 0:rim, :]
            edge = jnp.where(swap, head, tail) if near else jnp.where(swap, tail, head)
            pack[used : used + rim, c * LANES : (c + 1) * LANES] = edge
        target[...] = pack[...].astype(BF16)
    write.wait()


def back_rows(kernel, gain, w_in, d_conv, left, sig, x_norm, inv_norm, d_glu, d_normed, rows):
    n_taps, channels = kernel.shape
    model = w_in.shape[0]
    for c in range(channels // LANES):
        cols = slice(c * LANES, (c + 1) * LANES)
        acc = jnp.zeros((rows, LANES), F32)
        for t in range(n_taps):
            acc = acc + kernel[t : t + 1, cols] * d_conv(c, t)
        sg = sig(cols)
        d_left = acc * sg
        d_glu[:, cols] = d_left.astype(BF16)
        d_glu[:, channels + c * LANES : channels + (c + 1) * LANES] = (
            d_left * left(cols) * (1.0 - sg)
        ).astype(BF16)
    step = 256
    for n in range(model // step):
        d_normed[:, pl.ds(n * step, step)] = dot_t(d_glu[...], w_in[pl.ds(n * step, step), :])
    for r in range(0, rows, 32):
        g = d_normed[r : r + 32, :] * gain
        x = x_norm(r)
        yield r, (inv_norm(r) * (g - row_mean(g) - x * row_mean(g * x))).astype(BF16)


def inner_kernel(
    kernel, norm_gain, w_in, x_norm, inv_norm, left, sig, d_conv, sums, d_hidden, sums_out, d_glu,
    d_normed, out, sem,
):
    sums_out[...] = sums[...]
    rows = out.shape[0]
    rim = (kernel.shape[0] - 1) // 2
    blocks = back_rows(
        kernel, norm_gain[...], w_in,
        lambda c, t: d_conv[c, pl.ds(HALO + rim - t, rows), :],
        lambda cols: left[HALO : HALO + rows, cols],
        lambda cols: sig[HALO : HALO + rows, cols],
        lambda r: x_norm[2 * HALO + r : 2 * HALO + r + 32, :],
        lambda r: inv_norm[2 * HALO + r : 2 * HALO + r + 32, 0:1],
        d_glu, d_normed, rows,
    )
    for r, block in blocks:
        out[r : r + 32, :] = block
    write = pltpu.make_async_copy(out, d_hidden.at[pl.ds(HALO, rows), :], sem)
    write.start()
    write.wait()


def edge_kernel(
    pairwise, count, inner, from_b, from_a, kernel, norm_gain, w_in, x_norm, inv_norm, left, sig,
    d_conv, d_hidden, padded, edges, d_glu, d_normed, out, sem,
):
    frames, channels = left.shape
    n_taps = kernel.shape[0]
    rim = (n_taps - 1) // 2
    me = lax.axis_index("ctx")
    swap = swapped(pairwise)
    used = n_taps + 2
    edges[0] = from_a[...].astype(F32)
    edges[1] = from_b[...].astype(F32)
    for c in range(channels // LANES):
        cols = slice(c * LANES, (c + 1) * LANES)
        a, b = edges[0, used : used + rim, cols], edges[1, used : used + rim, cols]
        padded[0, c, HALO - rim : HALO, :] = jnp.where(me == 0, 0.0, jnp.where(swap, a, b))
        padded[0, c, HALO:, :] = d_conv[c, 0 : 2 * HALO, :]
        padded[1, c, 0 : 2 * HALO, :] = d_conv[c, frames - 2 * HALO :, :]
        padded[1, c, 2 * HALO : 2 * HALO + rim, :] = jnp.where(
            me == count - 1, 0.0, jnp.where(swap, b, a)
        )

    def both(ref, at, cols):
        low = ref[at : at + HALO, cols]
        return jnp.concatenate([low, ref[at + frames - HALO : at + frames, cols]], axis=0)

    def pick(c, t):
        rows = pl.ds(HALO + rim - t, HALO)
        return jnp.concatenate([padded[0, c, rows, :], padded[1, c, rows, :]], axis=0)

    every = slice(None)
    blocks = back_rows(
        kernel, norm_gain[...], w_in, pick,
        lambda cols: both(left, 0, cols), lambda cols: both(sig, 0, cols),
        lambda r: both(x_norm, HALO, every), lambda r: both(inv_norm, HALO, slice(0, 1)),
        d_glu, d_normed, 2 * HALO,
    )
    for r, block in blocks:
        out[...] = block
    writes = [
        pltpu.make_async_copy(
            out.at[pl.ds(i * HALO, HALO), :],
            d_hidden.at[pl.ds(i * (frames - HALO), HALO), :],
            sem.at[i],
        )
        for i in range(2)
    ]
    for write in writes:
        write.start()
    for write in writes:
        write.wait()


def total_kernel(factor, one, two, three, four, d_kernel, d_gain, d_bias):
    n_taps = d_kernel.shape[0]
    total = (one[...].astype(F32) + two[...].astype(F32)) + (
        three[...].astype(F32) + four[...].astype(F32)
    )
    total = total * factor
    d_kernel[...] = total[0:n_taps]
    d_gain[...] = total[n_taps : n_taps + 1]
    d_bias[...] = total[n_taps + 1 :]


def flips(array, axis, which):
    return [lax.ppermute(array, axis, [(i, i ^ k) for i in range(4)]) for k in which]


def to_neighbours(pairwise, count, to_a, to_b):
    if pairwise:
        return flips(to_a, "ctx", (1,)) + flips(to_b, "ctx", (3,))
    return [
        lax.ppermute(to_b, "ctx", [((i + 1) % count, i) for i in range(count)]),
        lax.ppermute(to_a, "ctx", [(i, (i + 1) % count) for i in range(count)]),
    ]


def per_device(
    resid, query, keys, values, w_out, norm_gain, w_in, kernel, conv_gain, conv_bias, cotangent
):
    frames, model = resid.shape[1:]
    width = query.shape[2]
    channels = cotangent.shape[2]
    n_taps = kernel.shape[0]
    rim = (n_taps - 1) // 2
    ctx, dp = lax.axis_size("ctx"), lax.axis_size("dp")
    pairwise = ctx == 4 and dp == 4
    resid, query, keys, values, cotangent = (
        x.reshape(x.shape[1:]) for x in (resid, query, keys, values, cotangent)
    )
    norm_gain, conv_gain, conv_bias = (x.reshape(1, -1) for x in (norm_gain, conv_gain, conv_bias))
    pooled = frames // POOL
    edge = HALO * (1 + model // width)
    n_edges = 2 * (1 + model // width)

    own, to_a, to_b = pl.pallas_call(
        functools.partial(pack_kernel, pairwise),
        out_shape=(
            shape((2 * pooled, width), BF16),
            shape((edge, width), BF16),
            shape((edge, width), BF16),
        ),
        in_specs=[HBM] * 4,
        out_specs=(VMEM,) * 3,
        scratch_shapes=[
            pltpu.VMEM((2, frames, width), BF16),
            pltpu.SemaphoreType.DMA((n_edges,)),
            pltpu.SemaphoreType.DMA((2,)),
        ],
        compiler_params=pltpu.CompilerParams(vmem_limit_bytes=4 * 2**20),
    )(*in_hbm(keys, values, query, resid))

    if pairwise:
        near, far, across = flips(own, "ctx", (1, 2, 3))
        (from_a,) = flips(to_a, "ctx", (1,))
        from_b = lax.ppermute(to_b, "ctx", [(1, 2), (2, 1)])
        kvs = (own, near, far, across)
        kv_places = ((0, pooled, pooled),) * 4
    else:
        from_a, from_b = to_neighbours(pairwise, ctx, to_a, to_b)
        kvs = tuple(
            lax.all_gather(part, "ctx", axis=0, tiled=True) for part in (own[:pooled], own[pooled:])
        )
        kv_places = ((0, None, pooled * ctx), (None, 0, pooled * ctx))

    operands = (
        query, resid, cotangent, w_out, norm_gain, w_in, kernel, conv_gain, conv_bias,
    )
    operands = pl.pallas_call(
        functools.partial(fetch_kernel, len(operands)),
        out_shape=tuple(shape(x.shape, x.dtype) for x in operands),
        in_specs=[HBM] * (1 + len(operands)),
        out_specs=(VMEM,) * len(operands),
        scratch_shapes=[pltpu.SemaphoreType.DMA((len(operands),))],
        compiler_params=pltpu.CompilerParams(vmem_limit_bytes=8 * 2**20),
    )(own, *in_hbm(*operands))
    norm_gain, w_in, kernel = operands[4:7]

    rows = frames + 2 * HALO
    used = n_taps + 2
    conv_act, x_norm, inv_norm, left, sig, d_conv, to_a, to_b, sums = pl.pallas_call(
        functools.partial(main_kernel, pairwise, ctx, kv_places),
        out_shape=(
            shape((frames, channels), BF16),
            shape((rows, model), F32),
            shape((rows, LANES), F32),
            shape((frames, channels), F32),
            shape((frames, channels), F32),
            shape((channels // LANES, frames, LANES), F32),
            shape((used + rim, channels), BF16),
            shape((used + rim, channels), BF16),
            shape((used, channels), BF16 if pairwise else F32),
        ),
        in_specs=[VMEM] * (11 + len(kvs)),
        out_specs=(HBM,) + (VMEM,) * 8,
        scratch_shapes=[
            pltpu.VMEM((rows, width), BF16),
            pltpu.VMEM((2 * HALO, model), BF16),
            pltpu.VMEM((pooled * ctx, width), BF16),
            pltpu.VMEM((pooled * ctx, width), BF16),
            pltpu.VMEM((rows, width), BF16),
            pltpu.VMEM((rows, model), F32),
            pltpu.VMEM((rows, model), BF16),
            pltpu.VMEM((channels // LANES, rows, LANES), F32),
            pltpu.VMEM((frames, channels), F32),
            pltpu.VMEM((rows, 2 * channels), F32),
            pltpu.VMEM((n_taps * 8, LANES), F32),
            pltpu.VMEM((frames, channels), BF16),
            pltpu.VMEM((used + rim, channels), F32),
            pltpu.SemaphoreType.DMA,
        ],
        compiler_params=pltpu.CompilerParams(vmem_limit_bytes=32 * 2**20),
    )(*operands, *kvs, from_b, from_a)

    inner = frames - 2 * HALO
    common = (kernel, norm_gain, w_in, x_norm, inv_norm, left, sig, d_conv)
    d_inner, same_sums = pl.pallas_call(
        inner_kernel,
        out_shape=(shape((frames, model), BF16), shape(sums.shape, sums.dtype)),
        in_specs=[VMEM] * 9,
        out_specs=(HBM, VMEM),
        scratch_shapes=[
            pltpu.VMEM((inner, 2 * channels), BF16),
            pltpu.VMEM((inner, model), F32),
            pltpu.VMEM((inner, model), BF16),
            pltpu.SemaphoreType.DMA,
        ],
        compiler_params=pltpu.CompilerParams(vmem_limit_bytes=16 * 2**20),
    )(*common, sums)
    if pairwise:
        (from_b,) = flips(to_b, "ctx", (3,))
        (far,) = flips(sums, "ctx", (2,))
        (from_a,) = flips(to_a, "ctx", (1,))
        near, across = (x[:used].astype(F32) for x in (from_a, from_b))
        sums = ((same_sums.astype(F32) + near) + (far.astype(F32) + across)).astype(BF16)
        parts = [sums] + flips(sums, "dp", (1, 2, 3))
    else:
        from_a, from_b = to_neighbours(pairwise, ctx, to_a, to_b)
        sums = same_sums

    d_hidden = pl.pallas_call(
        functools.partial(edge_kernel, pairwise, ctx),
        out_shape=shape((frames, model), BF16),
        in_specs=[HBM] + [VMEM] * 10,
        out_specs=HBM,
        input_output_aliases={0: 0},
        scratch_shapes=[
            pltpu.VMEM((2, channels // LANES, 3 * HALO, LANES), F32),
            pltpu.VMEM((2, used + rim, channels), F32),
            pltpu.VMEM((2 * HALO, 2 * channels), BF16),
            pltpu.VMEM((2 * HALO, model), F32),
            pltpu.VMEM((2 * HALO, model), BF16),
            pltpu.SemaphoreType.DMA((2,)),
        ],
        compiler_params=pltpu.CompilerParams(vmem_limit_bytes=16 * 2**20),
    )(d_inner, from_b, from_a, *common)

    factor = 1.0 / math.sqrt(frames * ctx * dp)
    if pairwise:
        d_kernel, d_gain, d_bias = pl.pallas_call(
            functools.partial(total_kernel, factor),
            out_shape=(shape((n_taps, channels), F32),) + (shape((1, channels), F32),) * 2,
            in_specs=[VMEM] * 4,
            out_specs=(VMEM,) * 3,
            compiler_params=pltpu.CompilerParams(vmem_limit_bytes=2 * 2**20),
        )(*parts)
        d_gain, d_bias = d_gain.reshape(-1), d_bias.reshape(-1)
    else:
        total = lax.psum(sums, ("ctx", "dp")) * factor
        d_kernel, d_gain, d_bias = total[:n_taps], total[n_taps], total[n_taps + 1]
    return (conv_act[None], d_hidden[None], d_kernel, d_gain, d_bias)


def solution(mesh):
    split = P(("groups", "dp"), "ctx", None)
    return jax.shard_map(
        per_device,
        mesh=mesh,
        in_specs=(split,) * 4 + (P(),) * 6 + (split,),
        out_specs=(split, split, P("groups", None), P("groups"), P("groups")),
        check_vma=False,
    )
```

```python
import functools
import math

import jax
import jax.numpy as jnp
from jax import lax
from jax.experimental import pallas as pl
from jax.experimental.pallas import tpu as pltpu
from jax.sharding import PartitionSpec as P

HEAD_DIM = 64
POOL = 4
EPSILON = 1e-05

LANES = 128
HALO = 16
F32 = jnp.float32
BF16 = jnp.bfloat16

VMEM = pl.BlockSpec(memory_space=pltpu.VMEM)
HBM = pl.BlockSpec(memory_space=pltpu.HBM)
shape = jax.ShapeDtypeStruct


def dot(a, b):
    return lax.dot_general(a, b, (((1,), (0,)), ((), ())), preferred_element_type=F32)


def dot_t(a, b):
    return lax.dot_general(a, b, (((1,), (1,)), ((), ())), preferred_element_type=F32)


def row_mean(x):
    return jnp.sum(x, axis=-1, keepdims=True) * (1.0 / x.shape[-1])


def in_hbm(*arrays):
    return [pltpu.with_memory_space_constraint(x, pltpu.HBM) for x in arrays]


def swapped(pairwise):
    return lax.rem(lax.axis_index("ctx"), 2) == 1 if pairwise else False


def pack_kernel(pairwise, keys, values, query, resid, own, to_a, to_b, kv, sem, kv_sem):
    frames, width = keys.shape
    model = resid.shape[1]
    pooled = frames // POOL
    swap = swapped(pairwise)
    loads = [
        pltpu.make_async_copy(source, kv.at[place], kv_sem.at[place])
        for place, source in enumerate((keys, values))
    ]
    for load in loads:
        load.start()
    edges = []
    for target, near in ((to_a, True), (to_b, False)):
        at = 2 * pooled
        start = jnp.where(swap, 0 if near else frames - HALO, frames - HALO if near else 0)
        start = pl.multiple_of(start.astype(jnp.int32), HALO)
        for source, column in [(query, 0)] + [(resid, c) for c in range(0, model, width)]:
            edges.append(
                pltpu.make_async_copy(
                    source.at[pl.ds(start, HALO), pl.ds(column, width)],
                    target.at[pl.ds(at, HALO), :],
                    sem.at[len(edges)],
                )
            )
            edges[-1].start()
            at += HALO
    row = lax.broadcasted_iota(jnp.int32, (pooled, frames), 0)
    col = lax.broadcasted_iota(jnp.int32, (pooled, frames), 1)
    mean = jnp.where(col // POOL == row, 1.0 / POOL, 0.0).astype(BF16)
    for place, load in enumerate(loads):
        load.wait()
        block = dot(mean, kv[place]).astype(BF16)
        rows = pl.ds(place * pooled, pooled)
        own[rows, :] = block
        to_a[rows, :] = block
        to_b[rows, :] = block
    for edge in edges:
        edge.wait()


def fetch_kernel(count, after, *refs):
    sources, targets, sem = refs[:count], refs[count : 2 * count], refs[2 * count]
    copies = [
        pltpu.make_async_copy(a, b, sem.at[i]) for i, (a, b) in enumerate(zip(sources, targets))
    ]
    for copy in copies:
        copy.start()
    for copy in copies:
        copy.wait()


def main_kernel(pairwise, count, n_kv, *refs):
    (query, resid, cotangent, w_out, norm_gain, w_in, kernel, conv_gain, conv_bias) = refs[:9]
    kvs = refs[9 : 9 + n_kv]
    from_b, from_a = refs[9 + n_kv : 11 + n_kv]
    (conv_act, x_norm, inv_norm, left_out, sig_out, d_conv) = refs[11 + n_kv : 17 + n_kv]
    to_a, to_b, sums = refs[17 + n_kv : 20 + n_kv]
    (q_all, r_edge, k_all, v_all, att, hid, normed, gated, conv, glu, taps, act_out, pack, sem) = (
        refs[20 + n_kv :]
    )
    frames, width = query.shape
    model = resid.shape[1]
    channels = w_in.shape[1] // 2
    rows = frames + 2 * HALO
    n_taps = kernel.shape[0]
    rim = (n_taps - 1) // 2
    me = lax.axis_index("ctx")
    first = me == 0
    last = me == count - 1
    swap = swapped(pairwise)
    main = pl.ds(HALO, frames)

    pooled = frames // POOL
    if pairwise:
        own, far, ends = kvs
        middle = (me == 1) | (me == 2)
        for side, target in enumerate((k_all, v_all)):
            rows_in = pl.ds(side * pooled, pooled)
            target[0:pooled, :] = own[rows_in, :]
            target[pooled : 2 * pooled, :] = from_a[rows_in, :]
            target[2 * pooled : 3 * pooled, :] = far[rows_in, :]
            target[3 * pooled :, :] = jnp.where(middle, from_b[rows_in, :], ends[rows_in, :])
    else:
        for source, target in zip(kvs, (k_all, v_all)):
            target[...] = source[...]
    keylen = count * pooled
    q_all[main, :] = query[...]
    for left_side in (True, False):
        edge_rows = pl.ds(0 if left_side else HALO + frames, HALO)
        r_rows = pl.ds(0 if left_side else HALO, HALO)

        def pick(start):
            a = from_a[pl.ds(2 * pooled + start, HALO), :]
            b = from_b[pl.ds(2 * pooled + start, HALO), :]
            return jnp.where(swap, a, b) if left_side else jnp.where(swap, b, a)

        q_all[edge_rows, :] = pick(0)
        for piece in range(model // width):
            r_edge[r_rows, pl.ds(piece * width, width)] = pick(HALO * (1 + piece))

    lane = lax.broadcasted_iota(jnp.int32, (keylen, LANES), 1)
    low = lane < HEAD_DIM
    zero = jnp.zeros((keylen, LANES), BF16)
    ones_low = jnp.where(low, 1.0, 0.0).astype(BF16)
    ones_high = jnp.where(low, 0.0, 1.0).astype(BF16)
    scale = 1.0 / math.sqrt(HEAD_DIM)
    for pair in range(width // LANES):
        cols = pl.ds(pair * LANES, LANES)
        k_pair = k_all[:, cols]
        v_pair = v_all[:, cols]
        q_pair = q_all[:, cols]
        weighted = None
        for keep_low in (True, False):
            k_head = jnp.where(low, k_pair, zero) if keep_low else jnp.where(low, zero, k_pair)
            v_head = jnp.where(low, v_pair, zero) if keep_low else jnp.where(low, zero, v_pair)
            ones = ones_low if keep_low else ones_high
            scores = dot_t(q_pair, k_head)
            top = jnp.max(scores, axis=-1, keepdims=True)
            probs = jnp.exp((scores - top) * scale).astype(BF16)
            part = dot(probs, jnp.concatenate([v_head, ones], axis=1))
            weighted = part if weighted is None else weighted + part
        att[:, cols] = (weighted[:, :LANES] / weighted[:, LANES:]).astype(BF16)

    step = 256
    for n in range(model // step):
        cols = pl.ds(n * step, step)
        out = dot(att[...], w_out[:, cols])
        for rows_in, res in (
            (slice(0, HALO), r_edge[0:HALO, cols]),
            (slice(HALO, HALO + frames), resid[:, cols]),
            (slice(HALO + frames, rows), r_edge[HALO:, cols]),
        ):
            hid[rows_in, cols] = (res.astype(F32) + out[rows_in]).astype(BF16).astype(F32)

    gain = norm_gain[...]
    for r in range(0, rows, 32):
        x = hid[r : r + 32, :]
        x = x - row_mean(x)
        inv = lax.rsqrt(row_mean(x * x) + EPSILON)
        x = x * inv
        normed[r : r + 32, :] = (x * gain).astype(BF16)
        x_norm[r : r + 32, :] = x
        inv_norm[r : r + 32, :] = jnp.broadcast_to(inv, (32, LANES))

    for n in range(2 * channels // step):
        cols = pl.ds(n * step, step)
        glu[:, cols] = dot(normed[...], w_in[:, cols])
    for r in range(0, rows, 16):
        left = glu[r : r + 16, 0:channels]
        sig = jax.nn.sigmoid(glu[r : r + 16, channels:])
        out = (left * sig).astype(BF16).astype(F32)
        if r < HALO:
            out = jnp.where(first, 0.0, out)
        elif r >= HALO + frames:
            out = jnp.where(last, 0.0, out)
        else:
            left_out[r - HALO : r - HALO + 16, :] = left
            sig_out[r - HALO : r - HALO + 16, :] = sig
        for c in range(channels // LANES):
            gated[c, r : r + 16, :] = out[:, c * LANES : (c + 1) * LANES]

    for c in range(channels // LANES):
        cols = slice(c * LANES, (c + 1) * LANES)
        acc = jnp.zeros((frames, LANES), F32)
        for t in range(n_taps):
            acc = acc + kernel[t : t + 1, cols] * gated[c, pl.ds(HALO + t - rim, frames), :]
        conv[:, cols] = acc

    gain = conv_gain[...]
    bias = conv_bias[...]
    sum_gain = jnp.zeros((8, channels), F32)
    sum_bias = jnp.zeros((8, channels), F32)
    for r in range(0, frames, 16):
        z = conv[r : r + 16, :]
        z = z - row_mean(z)
        inv = lax.rsqrt(row_mean(z * z) + EPSILON)
        z = z * inv
        act_in = z * gain + bias
        sig = jax.nn.sigmoid(act_in)
        act = act_in * sig
        act_out[r : r + 16, :] = act.astype(BF16)
        d_act = cotangent[r : r + 16, :].astype(F32) * (sig + act * (1.0 - sig))
        d_gain = d_act * z
        sum_gain = sum_gain + d_gain[:8] + d_gain[8:]
        sum_bias = sum_bias + d_act[:8] + d_act[8:]
        g = d_act * gain
        d = (inv * (g - row_mean(g) - z * row_mean(g * z))).astype(BF16).astype(F32)
        for c in range(channels // LANES):
            d_conv[c, r : r + 16, :] = d[:, c * LANES : (c + 1) * LANES]
    write = pltpu.make_async_copy(act_out, conv_act, sem)
    write.start()
    pack[n_taps : n_taps + 1, :] = jnp.sum(sum_gain, axis=0, keepdims=True)
    pack[n_taps + 1 : n_taps + 2, :] = jnp.sum(sum_bias, axis=0, keepdims=True)

    for c in range(channels // LANES):
        cols = slice(c * LANES, (c + 1) * LANES)
        accs = [jnp.zeros((8, LANES), F32) for _ in range(n_taps)]
        for r in range(0, frames, 8):
            d = d_conv[c, r : r + 8, :]
            for t in range(n_taps):
                accs[t] = accs[t] + d * gated[c, pl.ds(HALO + r + t - rim, 8), :]
        for t in range(n_taps):
            taps[t * 8 : t * 8 + 8, :] = accs[t]
        total = taps[pl.ds(0, n_taps, stride=8), :]
        for s in range(1, 8):
            total = total + taps[pl.ds(s, n_taps, stride=8), :]
        pack[0:n_taps, cols] = total

    used = n_taps + 2
    if pairwise:
        sums[...] = pack[0:used, :].astype(BF16)
    else:
        sums[...] = pack[0:used, :]
    for target, near in ((to_a, True), (to_b, False)):
        for c in range(channels // LANES):
            tail, head = d_conv[c, frames - rim :, :], d_conv[c, 0:rim, :]
            edge = jnp.where(swap, head, tail) if near else jnp.where(swap, tail, head)
            pack[used : used + rim, c * LANES : (c + 1) * LANES] = edge
        target[...] = pack[...].astype(BF16)
    write.wait()


def back_rows(kernel, gain, w_in, d_conv, left, sig, x_norm, inv_norm, d_glu, d_normed, rows):
    n_taps, channels = kernel.shape
    model = w_in.shape[0]
    for c in range(channels // LANES):
        cols = slice(c * LANES, (c + 1) * LANES)
        acc = jnp.zeros((rows, LANES), F32)
        for t in range(n_taps):
            acc = acc + kernel[t : t + 1, cols] * d_conv(c, t)
        sg = sig(cols)
        d_left = acc * sg
        d_glu[:, cols] = d_left.astype(BF16)
        d_glu[:, channels + c * LANES : channels + (c + 1) * LANES] = (
            d_left * left(cols) * (1.0 - sg)
        ).astype(BF16)
    step = 256
    for n in range(model // step):
        d_normed[:, pl.ds(n * step, step)] = dot_t(d_glu[...], w_in[pl.ds(n * step, step), :])
    for r in range(0, rows, 32):
        g = d_normed[r : r + 32, :] * gain
        x = x_norm(r)
        yield r, (inv_norm(r) * (g - row_mean(g) - x * row_mean(g * x))).astype(BF16)


def inner_kernel(
    kernel, norm_gain, w_in, x_norm, inv_norm, left, sig, d_conv, sums, d_hidden, sums_out, d_glu,
    d_normed, out, sem,
):
    sums_out[...] = sums[...]
    rows = out.shape[0]
    rim = (kernel.shape[0] - 1) // 2
    blocks = back_rows(
        kernel, norm_gain[...], w_in,
        lambda c, t: d_conv[c, pl.ds(HALO + rim - t, rows), :],
        lambda cols: left[HALO : HALO + rows, cols],
        lambda cols: sig[HALO : HALO + rows, cols],
        lambda r: x_norm[2 * HALO + r : 2 * HALO + r + 32, :],
        lambda r: inv_norm[2 * HALO + r : 2 * HALO + r + 32, 0:1],
        d_glu, d_normed, rows,
    )
    for r, block in blocks:
        out[r : r + 32, :] = block
    write = pltpu.make_async_copy(out, d_hidden.at[pl.ds(HALO, rows), :], sem)
    write.start()
    write.wait()


def edge_kernel(
    pairwise, count, inner, from_b, from_a, kernel, norm_gain, w_in, x_norm, inv_norm, left, sig,
    d_conv, d_hidden, padded, edges, d_glu, d_normed, out, sem,
):
    frames, channels = left.shape
    n_taps = kernel.shape[0]
    rim = (n_taps - 1) // 2
    me = lax.axis_index("ctx")
    swap = swapped(pairwise)
    used = n_taps + 2
    edges[0] = from_a[...].astype(F32)
    edges[1] = from_b[...].astype(F32)
    for c in range(channels // LANES):
        cols = slice(c * LANES, (c + 1) * LANES)
        a, b = edges[0, used : used + rim, cols], edges[1, used : used + rim, cols]
        padded[0, c, HALO - rim : HALO, :] = jnp.where(me == 0, 0.0, jnp.where(swap, a, b))
        padded[0, c, HALO:, :] = d_conv[c, 0 : 2 * HALO, :]
        padded[1, c, 0 : 2 * HALO, :] = d_conv[c, frames - 2 * HALO :, :]
        padded[1, c, 2 * HALO : 2 * HALO + rim, :] = jnp.where(
            me == count - 1, 0.0, jnp.where(swap, b, a)
        )

    def both(ref, at, cols):
        low = ref[at : at + HALO, cols]
        return jnp.concatenate([low, ref[at + frames - HALO : at + frames, cols]], axis=0)

    def pick(c, t):
        rows = pl.ds(HALO + rim - t, HALO)
        return jnp.concatenate([padded[0, c, rows, :], padded[1, c, rows, :]], axis=0)

    every = slice(None)
    blocks = back_rows(
        kernel, norm_gain[...], w_in, pick,
        lambda cols: both(left, 0, cols), lambda cols: both(sig, 0, cols),
        lambda r: both(x_norm, HALO, every), lambda r: both(inv_norm, HALO, slice(0, 1)),
        d_glu, d_normed, 2 * HALO,
    )
    for r, block in blocks:
        out[...] = block
    writes = [
        pltpu.make_async_copy(
            out.at[pl.ds(i * HALO, HALO), :],
            d_hidden.at[pl.ds(i * (frames - HALO), HALO), :],
            sem.at[i],
        )
        for i in range(2)
    ]
    for write in writes:
        write.start()
    for write in writes:
        write.wait()


def total_kernel(factor, one, two, three, four, d_kernel, d_gain, d_bias):
    n_taps = d_kernel.shape[0]
    total = (one[...].astype(F32) + two[...].astype(F32)) + (
        three[...].astype(F32) + four[...].astype(F32)
    )
    total = total * factor
    d_kernel[...] = total[0:n_taps]
    d_gain[...] = total[n_taps : n_taps + 1]
    d_bias[...] = total[n_taps + 1 :]


def flips(array, axis, which):
    return [lax.ppermute(array, axis, [(i, i ^ k) for i in range(4)]) for k in which]


def to_neighbours(pairwise, count, to_a, to_b):
    if pairwise:
        return flips(to_a, "ctx", (1,)) + flips(to_b, "ctx", (3,))
    return [
        lax.ppermute(to_b, "ctx", [((i + 1) % count, i) for i in range(count)]),
        lax.ppermute(to_a, "ctx", [(i, (i + 1) % count) for i in range(count)]),
    ]


def per_device(
    resid, query, keys, values, w_out, norm_gain, w_in, kernel, conv_gain, conv_bias, cotangent
):
    frames, model = resid.shape[1:]
    width = query.shape[2]
    channels = cotangent.shape[2]
    n_taps = kernel.shape[0]
    rim = (n_taps - 1) // 2
    ctx, dp = lax.axis_size("ctx"), lax.axis_size("dp")
    pairwise = ctx == 4 and dp == 4
    resid, query, keys, values, cotangent = (
        x.reshape(x.shape[1:]) for x in (resid, query, keys, values, cotangent)
    )
    norm_gain, conv_gain, conv_bias = (x.reshape(1, -1) for x in (norm_gain, conv_gain, conv_bias))
    pooled = frames // POOL
    message = 2 * pooled + HALO * (1 + model // width)
    n_edges = 2 * (1 + model // width)

    own, to_a, to_b = pl.pallas_call(
        functools.partial(pack_kernel, pairwise),
        out_shape=(
            shape((2 * pooled, width), BF16),
            shape((message, width), BF16),
            shape((message, width), BF16),
        ),
        in_specs=[HBM] * 4,
        out_specs=(VMEM,) * 3,
        scratch_shapes=[
            pltpu.VMEM((2, frames, width), BF16),
            pltpu.SemaphoreType.DMA((n_edges,)),
            pltpu.SemaphoreType.DMA((2,)),
        ],
        compiler_params=pltpu.CompilerParams(vmem_limit_bytes=4 * 2**20),
    )(*in_hbm(keys, values, query, resid))

    if pairwise:
        from_b = lax.ppermute(to_b, "ctx", [(1, 2), (2, 1)])
        (from_a,) = flips(to_a, "ctx", (1,))
        ends = lax.ppermute(own, "ctx", [(0, 3), (3, 0)])
        (far,) = flips(own, "ctx", (2,))
        kvs = (own, far, ends)
    else:
        from_a, from_b = to_neighbours(pairwise, ctx, to_a, to_b)
        kvs = tuple(
            lax.all_gather(part, "ctx", axis=0, tiled=True) for part in (own[:pooled], own[pooled:])
        )

    operands = (
        query, resid, cotangent, w_out, norm_gain, w_in, kernel, conv_gain, conv_bias,
    )
    operands = pl.pallas_call(
        functools.partial(fetch_kernel, len(operands)),
        out_shape=tuple(shape(x.shape, x.dtype) for x in operands),
        in_specs=[HBM] * (1 + len(operands)),
        out_specs=(VMEM,) * len(operands),
        scratch_shapes=[pltpu.SemaphoreType.DMA((len(operands),))],
        compiler_params=pltpu.CompilerParams(vmem_limit_bytes=8 * 2**20),
    )(own, *in_hbm(*operands))
    norm_gain, w_in, kernel = operands[4:7]

    rows = frames + 2 * HALO
    used = n_taps + 2
    conv_act, x_norm, inv_norm, left, sig, d_conv, to_a, to_b, sums = pl.pallas_call(
        functools.partial(main_kernel, pairwise, ctx, len(kvs)),
        out_shape=(
            shape((frames, channels), BF16),
            shape((rows, model), F32),
            shape((rows, LANES), F32),
            shape((frames, channels), F32),
            shape((frames, channels), F32),
            shape((channels // LANES, frames, LANES), F32),
            shape((used + rim, channels), BF16),
            shape((used + rim, channels), BF16),
            shape((used, channels), BF16 if pairwise else F32),
        ),
        in_specs=[VMEM] * (11 + len(kvs)),
        out_specs=(HBM,) + (VMEM,) * 8,
        scratch_shapes=[
            pltpu.VMEM((rows, width), BF16),
            pltpu.VMEM((2 * HALO, model), BF16),
            pltpu.VMEM((pooled * ctx, width), BF16),
            pltpu.VMEM((pooled * ctx, width), BF16),
            pltpu.VMEM((rows, width), BF16),
            pltpu.VMEM((rows, model), F32),
            pltpu.VMEM((rows, model), BF16),
            pltpu.VMEM((channels // LANES, rows, LANES), F32),
            pltpu.VMEM((frames, channels), F32),
            pltpu.VMEM((rows, 2 * channels), F32),
            pltpu.VMEM((n_taps * 8, LANES), F32),
            pltpu.VMEM((frames, channels), BF16),
            pltpu.VMEM((used + rim, channels), F32),
            pltpu.SemaphoreType.DMA,
        ],
        compiler_params=pltpu.CompilerParams(vmem_limit_bytes=32 * 2**20),
    )(*operands, *kvs, from_b, from_a)

    inner = frames - 2 * HALO
    common = (kernel, norm_gain, w_in, x_norm, inv_norm, left, sig, d_conv)
    d_inner, same_sums = pl.pallas_call(
        inner_kernel,
        out_shape=(shape((frames, model), BF16), shape(sums.shape, sums.dtype)),
        in_specs=[VMEM] * 9,
        out_specs=(HBM, VMEM),
        scratch_shapes=[
            pltpu.VMEM((inner, 2 * channels), BF16),
            pltpu.VMEM((inner, model), F32),
            pltpu.VMEM((inner, model), BF16),
            pltpu.SemaphoreType.DMA,
        ],
        compiler_params=pltpu.CompilerParams(vmem_limit_bytes=16 * 2**20),
    )(*common, sums)
    if pairwise:
        (from_b,) = flips(to_b, "ctx", (3,))
        (far,) = flips(sums, "ctx", (2,))
        (from_a,) = flips(to_a, "ctx", (1,))
        near, across = (x[:used].astype(F32) for x in (from_a, from_b))
        sums = ((same_sums.astype(F32) + near) + (far.astype(F32) + across)).astype(BF16)
        parts = [sums] + flips(sums, "dp", (1, 2, 3))
    else:
        from_a, from_b = to_neighbours(pairwise, ctx, to_a, to_b)
        sums = same_sums

    d_hidden = pl.pallas_call(
        functools.partial(edge_kernel, pairwise, ctx),
        out_shape=shape((frames, model), BF16),
        in_specs=[HBM] + [VMEM] * 10,
        out_specs=HBM,
        input_output_aliases={0: 0},
        scratch_shapes=[
            pltpu.VMEM((2, channels // LANES, 3 * HALO, LANES), F32),
            pltpu.VMEM((2, used + rim, channels), F32),
            pltpu.VMEM((2 * HALO, 2 * channels), BF16),
            pltpu.VMEM((2 * HALO, model), F32),
            pltpu.VMEM((2 * HALO, model), BF16),
            pltpu.SemaphoreType.DMA((2,)),
        ],
        compiler_params=pltpu.CompilerParams(vmem_limit_bytes=16 * 2**20),
    )(d_inner, from_b, from_a, *common)

    factor = 1.0 / math.sqrt(frames * ctx * dp)
    if pairwise:
        d_kernel, d_gain, d_bias = pl.pallas_call(
            functools.partial(total_kernel, factor),
            out_shape=(shape((n_taps, channels), F32),) + (shape((1, channels), F32),) * 2,
            in_specs=[VMEM] * 4,
            out_specs=(VMEM,) * 3,
            compiler_params=pltpu.CompilerParams(vmem_limit_bytes=2 * 2**20),
        )(*parts)
        d_gain, d_bias = d_gain.reshape(-1), d_bias.reshape(-1)
    else:
        total = lax.psum(sums, ("ctx", "dp")) * factor
        d_kernel, d_gain, d_bias = total[:n_taps], total[n_taps], total[n_taps + 1]
    return (conv_act[None], d_hidden[None], d_kernel, d_gain, d_bias)


def solution(mesh):
    split = P(("groups", "dp"), "ctx", None)
    return jax.shard_map(
        per_device,
        mesh=mesh,
        in_specs=(split,) * 4 + (P(),) * 6 + (split,),
        out_specs=(split, split, P("groups", None), P("groups"), P("groups")),
        check_vma=False,
    )
```

```python
import functools
import math

import jax
import jax.numpy as jnp
from jax import lax
from jax.experimental import pallas as pl
from jax.experimental.pallas import tpu as pltpu
from jax.sharding import PartitionSpec as P

HEAD_DIM = 64
POOL = 4
EPSILON = 1e-05

LANES = 128
HALO = 16
F32 = jnp.float32
BF16 = jnp.bfloat16

VMEM = pl.BlockSpec(memory_space=pltpu.VMEM)
HBM = pl.BlockSpec(memory_space=pltpu.HBM)
shape = jax.ShapeDtypeStruct


def dot(a, b):
    return lax.dot_general(a, b, (((1,), (0,)), ((), ())), preferred_element_type=F32)


def dot_t(a, b):
    return lax.dot_general(a, b, (((1,), (1,)), ((), ())), preferred_element_type=F32)


def row_mean(x):
    return jnp.sum(x, axis=-1, keepdims=True) * (1.0 / x.shape[-1])


def in_hbm(*arrays):
    return [pltpu.with_memory_space_constraint(x, pltpu.HBM) for x in arrays]


def swapped(pairwise):
    return lax.rem(lax.axis_index("ctx"), 2) == 1 if pairwise else False


def pack_kernel(pairwise, keys, values, query, resid, own, to_a, to_b, kv, sem, kv_sem):
    frames, width = keys.shape
    model = resid.shape[1]
    pooled = frames // POOL
    swap = swapped(pairwise)
    loads = [
        pltpu.make_async_copy(source, kv.at[place], kv_sem.at[place])
        for place, source in enumerate((keys, values))
    ]
    for load in loads:
        load.start()
    edges = []
    for target, near in ((to_a, True), (to_b, False)):
        at = 2 * pooled if near else 0
        start = jnp.where(swap, 0 if near else frames - HALO, frames - HALO if near else 0)
        start = pl.multiple_of(start.astype(jnp.int32), HALO)
        for source, column in [(query, 0)] + [(resid, c) for c in range(0, model, width)]:
            edges.append(
                pltpu.make_async_copy(
                    source.at[pl.ds(start, HALO), pl.ds(column, width)],
                    target.at[pl.ds(at, HALO), :],
                    sem.at[len(edges)],
                )
            )
            edges[-1].start()
            at += HALO
    row = lax.broadcasted_iota(jnp.int32, (pooled, frames), 0)
    col = lax.broadcasted_iota(jnp.int32, (pooled, frames), 1)
    mean = jnp.where(col // POOL == row, 1.0 / POOL, 0.0).astype(BF16)
    for place, load in enumerate(loads):
        load.wait()
        block = dot(mean, kv[place]).astype(BF16)
        rows = pl.ds(place * pooled, pooled)
        own[rows, :] = block
        to_a[rows, :] = block
    for edge in edges:
        edge.wait()


def fetch_kernel(count, after, *refs):
    sources, targets, sem = refs[:count], refs[count : 2 * count], refs[2 * count]
    copies = [
        pltpu.make_async_copy(a, b, sem.at[i]) for i, (a, b) in enumerate(zip(sources, targets))
    ]
    for copy in copies:
        copy.start()
    for copy in copies:
        copy.wait()


def main_kernel(pairwise, count, n_kv, *refs):
    (query, resid, cotangent, w_out, norm_gain, w_in, kernel, conv_gain, conv_bias) = refs[:9]
    kvs = refs[9 : 9 + n_kv]
    from_b, from_a = refs[9 + n_kv : 11 + n_kv]
    (conv_act, x_norm, inv_norm, left_out, sig_out, d_conv) = refs[11 + n_kv : 17 + n_kv]
    to_a, to_b, sums = refs[17 + n_kv : 20 + n_kv]
    (q_all, r_edge, k_all, v_all, att, hid, normed, gated, conv, glu, taps, act_out, pack, sem) = (
        refs[20 + n_kv :]
    )
    frames, width = query.shape
    model = resid.shape[1]
    channels = w_in.shape[1] // 2
    rows = frames + 2 * HALO
    n_taps = kernel.shape[0]
    rim = (n_taps - 1) // 2
    me = lax.axis_index("ctx")
    first = me == 0
    last = me == count - 1
    swap = swapped(pairwise)
    main = pl.ds(HALO, frames)

    pooled = frames // POOL
    if pairwise:
        own, far, across = kvs
        for side, target in enumerate((k_all, v_all)):
            rows_in = pl.ds(side * pooled, pooled)
            target[0:pooled, :] = own[rows_in, :]
            target[pooled : 2 * pooled, :] = from_a[rows_in, :]
            target[2 * pooled : 3 * pooled, :] = far[rows_in, :]
            target[3 * pooled :, :] = across[rows_in, :]
    else:
        for source, target in zip(kvs, (k_all, v_all)):
            target[...] = source[...]
    keylen = count * pooled
    q_all[main, :] = query[...]
    at_a = 2 * pooled if pairwise else 0
    for left_side in (True, False):
        edge_rows = pl.ds(0 if left_side else HALO + frames, HALO)
        r_rows = pl.ds(0 if left_side else HALO, HALO)

        def pick(start):
            a = from_a[pl.ds(at_a + start, HALO), :]
            b = from_b[pl.ds(start, HALO), :]
            return jnp.where(swap, a, b) if left_side else jnp.where(swap, b, a)

        q_all[edge_rows, :] = pick(0)
        for piece in range(model // width):
            r_edge[r_rows, pl.ds(piece * width, width)] = pick(HALO * (1 + piece))

    lane = lax.broadcasted_iota(jnp.int32, (keylen, LANES), 1)
    low = lane < HEAD_DIM
    zero = jnp.zeros((keylen, LANES), BF16)
    ones_low = jnp.where(low, 1.0, 0.0).astype(BF16)
    ones_high = jnp.where(low, 0.0, 1.0).astype(BF16)
    scale = 1.0 / math.sqrt(HEAD_DIM)
    pairs = width // LANES

    def score(pair):
        cols = pl.ds(pair * LANES, LANES)
        k_pair = k_all[:, cols]
        k_both = jnp.concatenate([jnp.where(low, k_pair, zero), jnp.where(low, zero, k_pair)], axis=0)
        return dot_t(q_all[:, cols], k_both)

    upcoming = score(0)
    for pair in range(pairs):
        cols = pl.ds(pair * LANES, LANES)
        scores = upcoming
        if pair + 1 < pairs:
            upcoming = score(pair + 1)
        v_pair = v_all[:, cols]
        probs = []
        for half in (scores[:, :keylen], scores[:, keylen:]):
            top = jnp.max(half, axis=-1, keepdims=True)
            probs.append(jnp.exp((half - top) * scale).astype(BF16))
        v_both = jnp.concatenate(
            [
                jnp.concatenate([jnp.where(low, v_pair, zero), ones_low], axis=1),
                jnp.concatenate([jnp.where(low, zero, v_pair), ones_high], axis=1),
            ],
            axis=0,
        )
        weighted = dot(jnp.concatenate(probs, axis=1), v_both)
        att[:, cols] = (weighted[:, :LANES] / weighted[:, LANES:]).astype(BF16)

    step = 256
    for n in range(model // step):
        cols = pl.ds(n * step, step)
        out = dot(att[...], w_out[:, cols])
        for rows_in, res in (
            (slice(0, HALO), r_edge[0:HALO, cols]),
            (slice(HALO, HALO + frames), resid[:, cols]),
            (slice(HALO + frames, rows), r_edge[HALO:, cols]),
        ):
            hid[rows_in, cols] = (res.astype(F32) + out[rows_in]).astype(BF16).astype(F32)

    gain = norm_gain[...]
    for r in range(0, rows, 32):
        x = hid[r : r + 32, :]
        x = x - row_mean(x)
        inv = lax.rsqrt(row_mean(x * x) + EPSILON)
        x = x * inv
        normed[r : r + 32, :] = (x * gain).astype(BF16)
        x_norm[r : r + 32, :] = x
        inv_norm[r : r + 32, :] = jnp.broadcast_to(inv, (32, LANES))

    def project(c):
        pair = [w_in[:, at + c * LANES : at + (c + 1) * LANES] for at in (0, channels)]
        glu[c] = dot(normed[...], jnp.concatenate(pair, axis=1))

    project(0)
    for c in range(channels // LANES):
        cols = slice(c * LANES, (c + 1) * LANES)
        if (c + 1) * LANES < channels:
            project(c + 1)
        for r in range(0, rows, 16):
            left = glu[c, r : r + 16, 0:LANES]
            sig = jax.nn.sigmoid(glu[c, r : r + 16, LANES:])
            out = (left * sig).astype(BF16).astype(F32)
            if r < HALO:
                out = jnp.where(first, 0.0, out)
            elif r >= HALO + frames:
                out = jnp.where(last, 0.0, out)
            else:
                left_out[r - HALO : r - HALO + 16, cols] = left
                sig_out[r - HALO : r - HALO + 16, cols] = sig
            gated[c, r : r + 16, :] = out
        acc = jnp.zeros((frames, LANES), F32)
        for t in range(n_taps):
            acc = acc + kernel[t : t + 1, cols] * gated[c, pl.ds(HALO + t - rim, frames), :]
        conv[:, cols] = acc

    gain = conv_gain[...]
    bias = conv_bias[...]
    sum_gain = jnp.zeros((8, channels), F32)
    sum_bias = jnp.zeros((8, channels), F32)
    for r in range(0, frames, 16):
        z = conv[r : r + 16, :]
        z = z - row_mean(z)
        inv = lax.rsqrt(row_mean(z * z) + EPSILON)
        z = z * inv
        act_in = z * gain + bias
        sig = jax.nn.sigmoid(act_in)
        act = act_in * sig
        act_out[r : r + 16, :] = act.astype(BF16)
        d_act = cotangent[r : r + 16, :].astype(F32) * (sig + act * (1.0 - sig))
        d_gain = d_act * z
        sum_gain = sum_gain + d_gain[:8] + d_gain[8:]
        sum_bias = sum_bias + d_act[:8] + d_act[8:]
        g = d_act * gain
        d = (inv * (g - row_mean(g) - z * row_mean(g * z))).astype(BF16).astype(F32)
        for c in range(channels // LANES):
            d_conv[c, r : r + 16, :] = d[:, c * LANES : (c + 1) * LANES]
    write = pltpu.make_async_copy(act_out, conv_act, sem)
    write.start()
    pack[n_taps : n_taps + 1, :] = jnp.sum(sum_gain, axis=0, keepdims=True)
    pack[n_taps + 1 : n_taps + 2, :] = jnp.sum(sum_bias, axis=0, keepdims=True)

    for c in range(channels // LANES):
        cols = slice(c * LANES, (c + 1) * LANES)
        accs = [jnp.zeros((8, LANES), F32) for _ in range(n_taps)]
        for r in range(0, frames, 8):
            d = d_conv[c, r : r + 8, :]
            for t in range(n_taps):
                accs[t] = accs[t] + d * gated[c, pl.ds(HALO + r + t - rim, 8), :]
        for t in range(n_taps):
            taps[t * 8 : t * 8 + 8, :] = accs[t]
        total = taps[pl.ds(0, n_taps, stride=8), :]
        for s in range(1, 8):
            total = total + taps[pl.ds(s, n_taps, stride=8), :]
        pack[0:n_taps, cols] = total

    used = n_taps + 2
    if pairwise:
        sums[...] = pack[0:used, :].astype(BF16)
    else:
        sums[...] = pack[0:used, :]
    for target, near in ((to_a, True), (to_b, False)):
        for c in range(channels // LANES):
            tail, head = d_conv[c, frames - rim :, :], d_conv[c, 0:rim, :]
            edge = jnp.where(swap, head, tail) if near else jnp.where(swap, tail, head)
            pack[used : used + rim, c * LANES : (c + 1) * LANES] = edge
        target[...] = pack[...].astype(BF16)
    write.wait()


def back_rows(kernel, gain, w_in, d_conv, left, sig, x_norm, inv_norm, d_glu, d_normed, rows):
    n_taps, channels = kernel.shape
    model = w_in.shape[0]
    for c in range(channels // LANES):
        cols = slice(c * LANES, (c + 1) * LANES)
        acc = jnp.zeros((rows, LANES), F32)
        for t in range(n_taps):
            acc = acc + kernel[t : t + 1, cols] * d_conv(c, t)
        sg = sig(cols)
        d_left = acc * sg
        d_glu[:, cols] = d_left.astype(BF16)
        d_glu[:, channels + c * LANES : channels + (c + 1) * LANES] = (
            d_left * left(cols) * (1.0 - sg)
        ).astype(BF16)
    step = 256
    for n in range(model // step):
        d_normed[:, pl.ds(n * step, step)] = dot_t(d_glu[...], w_in[pl.ds(n * step, step), :])
    for r in range(0, rows, 32):
        g = d_normed[r : r + 32, :] * gain
        x = x_norm(r)
        yield r, (inv_norm(r) * (g - row_mean(g) - x * row_mean(g * x))).astype(BF16)


def inner_kernel(
    kernel, norm_gain, w_in, x_norm, inv_norm, left, sig, d_conv, sums, out, sums_out, d_glu,
    d_normed,
):
    sums_out[...] = sums[...]
    rows = out.shape[0]
    rim = (kernel.shape[0] - 1) // 2
    blocks = back_rows(
        kernel, norm_gain[...], w_in,
        lambda c, t: d_conv[c, pl.ds(HALO + rim - t, rows), :],
        lambda cols: left[HALO : HALO + rows, cols],
        lambda cols: sig[HALO : HALO + rows, cols],
        lambda r: x_norm[2 * HALO + r : 2 * HALO + r + 32, :],
        lambda r: inv_norm[2 * HALO + r : 2 * HALO + r + 32, 0:1],
        d_glu, d_normed, rows,
    )
    for r, block in blocks:
        out[r : r + 32, :] = block


def edge_kernel(
    pairwise, count, inner, from_b, from_a, kernel, norm_gain, w_in, x_norm, inv_norm, left, sig,
    d_conv, d_hidden, padded, edges, d_glu, d_normed, out, sem,
):
    frames, channels = left.shape
    n_taps = kernel.shape[0]
    rim = (n_taps - 1) // 2
    me = lax.axis_index("ctx")
    swap = swapped(pairwise)
    used = n_taps + 2
    writes = [pltpu.make_async_copy(inner, d_hidden.at[pl.ds(HALO, inner.shape[0]), :], sem.at[2])]
    writes[0].start()
    edges[0] = from_a[...].astype(F32)
    edges[1] = from_b[...].astype(F32)
    for c in range(channels // LANES):
        cols = slice(c * LANES, (c + 1) * LANES)
        a, b = edges[0, used : used + rim, cols], edges[1, used : used + rim, cols]
        padded[0, c, HALO - rim : HALO, :] = jnp.where(me == 0, 0.0, jnp.where(swap, a, b))
        padded[0, c, HALO:, :] = d_conv[c, 0 : 2 * HALO, :]
        padded[1, c, 0 : 2 * HALO, :] = d_conv[c, frames - 2 * HALO :, :]
        padded[1, c, 2 * HALO : 2 * HALO + rim, :] = jnp.where(
            me == count - 1, 0.0, jnp.where(swap, b, a)
        )

    def both(ref, at, cols):
        low = ref[at : at + HALO, cols]
        return jnp.concatenate([low, ref[at + frames - HALO : at + frames, cols]], axis=0)

    def pick(c, t):
        rows = pl.ds(HALO + rim - t, HALO)
        return jnp.concatenate([padded[0, c, rows, :], padded[1, c, rows, :]], axis=0)

    every = slice(None)
    blocks = back_rows(
        kernel, norm_gain[...], w_in, pick,
        lambda cols: both(left, 0, cols), lambda cols: both(sig, 0, cols),
        lambda r: both(x_norm, HALO, every), lambda r: both(inv_norm, HALO, slice(0, 1)),
        d_glu, d_normed, 2 * HALO,
    )
    for r, block in blocks:
        out[...] = block
    writes += [
        pltpu.make_async_copy(
            out.at[pl.ds(i * HALO, HALO), :],
            d_hidden.at[pl.ds(i * (frames - HALO), HALO), :],
            sem.at[i],
        )
        for i in range(2)
    ]
    for write in writes[1:]:
        write.start()
    for write in writes:
        write.wait()


def total_kernel(factor, one, two, three, four, d_kernel, d_gain, d_bias):
    n_taps = d_kernel.shape[0]
    total = (one[...].astype(F32) + two[...].astype(F32)) + (
        three[...].astype(F32) + four[...].astype(F32)
    )
    total = total * factor
    d_kernel[...] = total[0:n_taps]
    d_gain[...] = total[n_taps : n_taps + 1]
    d_bias[...] = total[n_taps + 1 :]


def flips(array, axis, which):
    return [lax.ppermute(array, axis, [(i, i ^ k) for i in range(4)]) for k in which]


def to_neighbours(pairwise, count, to_a, to_b):
    if pairwise:
        return flips(to_a, "ctx", (1,)) + flips(to_b, "ctx", (3,))
    return [
        lax.ppermute(to_b, "ctx", [((i + 1) % count, i) for i in range(count)]),
        lax.ppermute(to_a, "ctx", [(i, (i + 1) % count) for i in range(count)]),
    ]


def per_device(
    resid, query, keys, values, w_out, norm_gain, w_in, kernel, conv_gain, conv_bias, cotangent
):
    frames, model = resid.shape[1:]
    width = query.shape[2]
    channels = cotangent.shape[2]
    n_taps = kernel.shape[0]
    rim = (n_taps - 1) // 2
    ctx, dp = lax.axis_size("ctx"), lax.axis_size("dp")
    pairwise = ctx == 4 and dp == 4
    resid, query, keys, values, cotangent = (
        x.reshape(x.shape[1:]) for x in (resid, query, keys, values, cotangent)
    )
    norm_gain, conv_gain, conv_bias = (x.reshape(1, -1) for x in (norm_gain, conv_gain, conv_bias))
    pooled = frames // POOL
    message = 2 * pooled + HALO * (1 + model // width)
    n_edges = 2 * (1 + model // width)

    own, to_a, to_b = pl.pallas_call(
        functools.partial(pack_kernel, pairwise),
        out_shape=(
            shape((2 * pooled, width), BF16),
            shape((message, width), BF16),
            shape((message - 2 * pooled, width), BF16),
        ),
        in_specs=[HBM] * 4,
        out_specs=(VMEM,) * 3,
        scratch_shapes=[
            pltpu.VMEM((2, frames, width), BF16),
            pltpu.SemaphoreType.DMA((n_edges,)),
            pltpu.SemaphoreType.DMA((2,)),
        ],
        compiler_params=pltpu.CompilerParams(vmem_limit_bytes=4 * 2**20),
    )(*in_hbm(keys, values, query, resid))

    if pairwise:
        (from_a,) = flips(to_a, "ctx", (1,))
        far, across = flips(own, "ctx", (2, 3))
        from_b = lax.ppermute(to_b, "ctx", [(1, 2), (2, 1)])
        kvs = (own, far, across)
    else:
        from_a, from_b = to_neighbours(pairwise, ctx, to_a[2 * pooled :], to_b)
        kvs = tuple(
            lax.all_gather(part, "ctx", axis=0, tiled=True) for part in (own[:pooled], own[pooled:])
        )

    operands = (
        query, resid, cotangent, w_out, norm_gain, w_in, kernel, conv_gain, conv_bias,
    )
    operands = pl.pallas_call(
        functools.partial(fetch_kernel, len(operands)),
        out_shape=tuple(shape(x.shape, x.dtype) for x in operands),
        in_specs=[HBM] * (1 + len(operands)),
        out_specs=(VMEM,) * len(operands),
        scratch_shapes=[pltpu.SemaphoreType.DMA((len(operands),))],
        compiler_params=pltpu.CompilerParams(vmem_limit_bytes=8 * 2**20),
    )(own, *in_hbm(*operands))
    norm_gain, w_in, kernel = operands[4:7]

    rows = frames + 2 * HALO
    used = n_taps + 2
    conv_act, x_norm, inv_norm, left, sig, d_conv, to_a, to_b, sums = pl.pallas_call(
        functools.partial(main_kernel, pairwise, ctx, len(kvs)),
        out_shape=(
            shape((frames, channels), BF16),
            shape((rows, model), F32),
            shape((rows, LANES), F32),
            shape((frames, channels), F32),
            shape((frames, channels), F32),
            shape((channels // LANES, frames, LANES), F32),
            shape((used + rim, channels), BF16),
            shape((used + rim, channels), BF16),
            shape((used, channels), BF16 if pairwise else F32),
        ),
        in_specs=[VMEM] * (11 + len(kvs)),
        out_specs=(HBM,) + (VMEM,) * 8,
        scratch_shapes=[
            pltpu.VMEM((rows, width), BF16),
            pltpu.VMEM((2 * HALO, model), BF16),
            pltpu.VMEM((pooled * ctx, width), BF16),
            pltpu.VMEM((pooled * ctx, width), BF16),
            pltpu.VMEM((rows, width), BF16),
            pltpu.VMEM((rows, model), F32),
            pltpu.VMEM((rows, model), BF16),
            pltpu.VMEM((channels // LANES, rows, LANES), F32),
            pltpu.VMEM((frames, channels), F32),
            pltpu.VMEM((channels // LANES, rows, 2 * LANES), F32),
            pltpu.VMEM((n_taps * 8, LANES), F32),
            pltpu.VMEM((frames, channels), BF16),
            pltpu.VMEM((used + rim, channels), F32),
            pltpu.SemaphoreType.DMA,
        ],
        compiler_params=pltpu.CompilerParams(vmem_limit_bytes=32 * 2**20),
    )(*operands, *kvs, from_b, from_a)

    inner = frames - 2 * HALO
    common = (kernel, norm_gain, w_in, x_norm, inv_norm, left, sig, d_conv)
    d_inner, same_sums = pl.pallas_call(
        inner_kernel,
        out_shape=(shape((inner, model), BF16), shape(sums.shape, sums.dtype)),
        in_specs=[VMEM] * 9,
        out_specs=(VMEM, VMEM),
        scratch_shapes=[
            pltpu.VMEM((inner, 2 * channels), BF16),
            pltpu.VMEM((inner, model), F32),
        ],
        compiler_params=pltpu.CompilerParams(vmem_limit_bytes=16 * 2**20),
    )(*common, sums)
    if pairwise:
        (from_b,) = flips(to_b, "ctx", (3,))
        (far,) = flips(sums, "ctx", (2,))
        (from_a,) = flips(to_a, "ctx", (1,))
        near, across = (x[:used].astype(F32) for x in (from_a, from_b))
        sums = ((same_sums.astype(F32) + near) + (far.astype(F32) + across)).astype(BF16)
        parts = [sums] + flips(sums, "dp", (1, 2, 3))
    else:
        from_a, from_b = to_neighbours(pairwise, ctx, to_a, to_b)
        sums = same_sums

    d_hidden = pl.pallas_call(
        functools.partial(edge_kernel, pairwise, ctx),
        out_shape=shape((frames, model), BF16),
        in_specs=[VMEM] * 11,
        out_specs=HBM,
        scratch_shapes=[
            pltpu.VMEM((2, channels // LANES, 3 * HALO, LANES), F32),
            pltpu.VMEM((2, used + rim, channels), F32),
            pltpu.VMEM((2 * HALO, 2 * channels), BF16),
            pltpu.VMEM((2 * HALO, model), F32),
            pltpu.VMEM((2 * HALO, model), BF16),
            pltpu.SemaphoreType.DMA((3,)),
        ],
        compiler_params=pltpu.CompilerParams(vmem_limit_bytes=16 * 2**20),
    )(d_inner, from_b, from_a, *common)

    factor = 1.0 / math.sqrt(frames * ctx * dp)
    if pairwise:
        d_kernel, d_gain, d_bias = pl.pallas_call(
            functools.partial(total_kernel, factor),
            out_shape=(shape((n_taps, channels), F32),) + (shape((1, channels), F32),) * 2,
            in_specs=[VMEM] * 4,
            out_specs=(VMEM,) * 3,
            compiler_params=pltpu.CompilerParams(vmem_limit_bytes=2 * 2**20),
        )(*parts)
        d_gain, d_bias = d_gain.reshape(-1), d_bias.reshape(-1)
    else:
        total = lax.psum(sums, ("ctx", "dp")) * factor
        d_kernel, d_gain, d_bias = total[:n_taps], total[n_taps], total[n_taps + 1]
    return (conv_act[None], d_hidden[None], d_kernel, d_gain, d_bias)


def solution(mesh):
    split = P(("groups", "dp"), "ctx", None)
    return jax.shard_map(
        per_device,
        mesh=mesh,
        in_specs=(split,) * 4 + (P(),) * 6 + (split,),
        out_specs=(split, split, P("groups", None), P("groups"), P("groups")),
        check_vma=False,
    )
```

```python
import functools
import math

import jax
import jax.numpy as jnp
from jax import lax
from jax.experimental import pallas as pl
from jax.experimental.pallas import tpu as pltpu
from jax.sharding import PartitionSpec as P

HEAD_DIM = 64
POOL = 4
EPSILON = 1e-05

LANES = 128
HALO = 16
F32 = jnp.float32
BF16 = jnp.bfloat16

VMEM = pl.BlockSpec(memory_space=pltpu.VMEM)
HBM = pl.BlockSpec(memory_space=pltpu.HBM)
shape = jax.ShapeDtypeStruct


def dot(a, b):
    return lax.dot_general(a, b, (((1,), (0,)), ((), ())), preferred_element_type=F32)


def dot_t(a, b):
    return lax.dot_general(a, b, (((1,), (1,)), ((), ())), preferred_element_type=F32)


def row_mean(x):
    return jnp.sum(x, axis=-1, keepdims=True) * (1.0 / x.shape[-1])


def in_hbm(*arrays):
    return [pltpu.with_memory_space_constraint(x, pltpu.HBM) for x in arrays]


def swapped(pairwise):
    return lax.rem(lax.axis_index("ctx"), 2) == 1 if pairwise else False


def pack_kernel(pairwise, keys, values, query, resid, own, to_a, to_b, kv, sem, kv_sem):
    frames, width = keys.shape
    model = resid.shape[1]
    pooled = frames // POOL
    swap = swapped(pairwise)
    loads = [
        pltpu.make_async_copy(source, kv.at[place], kv_sem.at[place])
        for place, source in enumerate((keys, values))
    ]
    for load in loads:
        load.start()
    edges = []
    for target, near in ((to_a, True), (to_b, False)):
        at = 2 * pooled if near else 0
        start = jnp.where(swap, 0 if near else frames - HALO, frames - HALO if near else 0)
        start = pl.multiple_of(start.astype(jnp.int32), HALO)
        for source, column in [(query, 0)] + [(resid, c) for c in range(0, model, width)]:
            edges.append(
                pltpu.make_async_copy(
                    source.at[pl.ds(start, HALO), pl.ds(column, width)],
                    target.at[pl.ds(at, HALO), :],
                    sem.at[len(edges)],
                )
            )
            edges[-1].start()
            at += HALO
    row = lax.broadcasted_iota(jnp.int32, (pooled, frames), 0)
    col = lax.broadcasted_iota(jnp.int32, (pooled, frames), 1)
    mean = jnp.where(col // POOL == row, 1.0 / POOL, 0.0).astype(BF16)
    for place, load in enumerate(loads):
        load.wait()
        block = dot(mean, kv[place]).astype(BF16)
        rows = pl.ds(place * pooled, pooled)
        own[rows, :] = block
        to_a[rows, :] = block
    for edge in edges:
        edge.wait()


def fetch_kernel(count, after, *refs):
    sources, targets, sem = refs[:count], refs[count : 2 * count], refs[2 * count]
    copies = [
        pltpu.make_async_copy(a, b, sem.at[i]) for i, (a, b) in enumerate(zip(sources, targets))
    ]
    for copy in copies:
        copy.start()
    for copy in copies:
        copy.wait()


def main_kernel(pairwise, count, n_kv, *refs):
    (query, resid, cotangent, w_out, norm_gain, w_in, kernel, conv_gain, conv_bias) = refs[:9]
    kvs = refs[9 : 9 + n_kv]
    from_b, from_a = refs[9 + n_kv : 11 + n_kv]
    (conv_act, x_norm, inv_norm, left_out, sig_out, d_conv) = refs[11 + n_kv : 17 + n_kv]
    to_a, to_b, sums = refs[17 + n_kv : 20 + n_kv]
    (q_all, r_edge, k_all, v_all, att, hid, normed, gated, conv, glu, taps, act_out, pack, sem) = (
        refs[20 + n_kv :]
    )
    frames, width = query.shape
    model = resid.shape[1]
    channels = w_in.shape[1] // 2
    rows = frames + 2 * HALO
    n_taps = kernel.shape[0]
    rim = (n_taps - 1) // 2
    me = lax.axis_index("ctx")
    first = me == 0
    last = me == count - 1
    swap = swapped(pairwise)
    main = pl.ds(HALO, frames)

    pooled = frames // POOL
    if pairwise:
        own, far, across = kvs
        for side, target in enumerate((k_all, v_all)):
            rows_in = pl.ds(side * pooled, pooled)
            target[0:pooled, :] = own[rows_in, :]
            target[pooled : 2 * pooled, :] = from_a[rows_in, :]
            target[2 * pooled : 3 * pooled, :] = far[rows_in, :]
            target[3 * pooled :, :] = across[rows_in, :]
    else:
        for source, target in zip(kvs, (k_all, v_all)):
            target[...] = source[...]
    keylen = count * pooled
    q_all[main, :] = query[...]
    at_a = 2 * pooled if pairwise else 0
    for left_side in (True, False):
        edge_rows = pl.ds(0 if left_side else HALO + frames, HALO)
        r_rows = pl.ds(0 if left_side else HALO, HALO)

        def pick(start):
            a = from_a[pl.ds(at_a + start, HALO), :]
            b = from_b[pl.ds(start, HALO), :]
            return jnp.where(swap, a, b) if left_side else jnp.where(swap, b, a)

        q_all[edge_rows, :] = pick(0)
        for piece in range(model // width):
            r_edge[r_rows, pl.ds(piece * width, width)] = pick(HALO * (1 + piece))

    lane = lax.broadcasted_iota(jnp.int32, (keylen, LANES), 1)
    low = lane < HEAD_DIM
    zero = jnp.zeros((keylen, LANES), BF16)
    ones_low = jnp.where(low, 1.0, 0.0).astype(BF16)
    ones_high = jnp.where(low, 0.0, 1.0).astype(BF16)
    scale = 1.0 / math.sqrt(HEAD_DIM)
    pairs = width // LANES

    def score(pair):
        cols = pl.ds(pair * LANES, LANES)
        k_pair = k_all[:, cols]
        k_both = jnp.concatenate([jnp.where(low, k_pair, zero), jnp.where(low, zero, k_pair)], axis=0)
        return dot_t(q_all[:, cols], k_both)

    upcoming = score(0)
    for pair in range(pairs):
        cols = pl.ds(pair * LANES, LANES)
        scores = upcoming
        if pair + 1 < pairs:
            upcoming = score(pair + 1)
        v_pair = v_all[:, cols]
        probs = []
        for half in (scores[:, :keylen], scores[:, keylen:]):
            top = jnp.max(half, axis=-1, keepdims=True)
            probs.append(jnp.exp((half - top) * scale).astype(BF16))
        v_both = jnp.concatenate(
            [
                jnp.concatenate([jnp.where(low, v_pair, zero), ones_low], axis=1),
                jnp.concatenate([jnp.where(low, zero, v_pair), ones_high], axis=1),
            ],
            axis=0,
        )
        weighted = dot(jnp.concatenate(probs, axis=1), v_both)
        att[:, cols] = (weighted[:, :LANES] / weighted[:, LANES:]).astype(BF16)

    step = 256
    for n in range(model // step):
        cols = pl.ds(n * step, step)
        out = dot(att[...], w_out[:, cols])
        for rows_in, res in (
            (slice(0, HALO), r_edge[0:HALO, cols]),
            (slice(HALO, HALO + frames), resid[:, cols]),
            (slice(HALO + frames, rows), r_edge[HALO:, cols]),
        ):
            hid[rows_in, cols] = (res.astype(F32) + out[rows_in]).astype(BF16).astype(F32)

    gain = norm_gain[...]
    for r in range(0, rows, 16):
        x = hid[r : r + 16, :]
        x = x - row_mean(x)
        inv = lax.rsqrt(row_mean(x * x) + EPSILON)
        x = x * inv
        normed[r : r + 16, :] = (x * gain).astype(BF16)
        x_norm[r : r + 16, :] = x
        inv_norm[r : r + 16, :] = jnp.broadcast_to(inv, (16, LANES))

    def project(c):
        pair = [w_in[:, at + c * LANES : at + (c + 1) * LANES] for at in (0, channels)]
        glu[c] = dot(normed[...], jnp.concatenate(pair, axis=1))

    offsets = [divmod(HALO + t - rim, 8) for t in range(n_taps)]
    by_offset = [
        (at, [(q, t) for t, (q, s) in enumerate(offsets) if s == at]) for at in range(8)
    ]
    project(0)
    for c in range(channels // LANES):
        cols = slice(c * LANES, (c + 1) * LANES)
        if (c + 1) * LANES < channels:
            project(c + 1)
        for r in range(0, rows, 16):
            left = glu[c, r : r + 16, 0:LANES]
            sig = jax.nn.sigmoid(glu[c, r : r + 16, LANES:])
            out = (left * sig).astype(BF16).astype(F32)
            if r < HALO:
                out = jnp.where(first, 0.0, out)
            elif r >= HALO + frames:
                out = jnp.where(last, 0.0, out)
            else:
                left_out[r - HALO : r - HALO + 16, cols] = left
                sig_out[r - HALO : r - HALO + 16, cols] = sig
            gated[c, r : r + 16, :] = out
        accs = [jnp.zeros((8, LANES), F32) for _ in range(frames // 8)]
        for at, taps_at in by_offset:
            spread = {q: jnp.broadcast_to(kernel[t : t + 1, cols], (8, LANES)) for q, t in taps_at}
            for j in range(frames // 8 + 3):
                tile = gated[c, pl.ds(8 * j + at, 8), :]
                for q, _ in taps_at:
                    if 0 <= j - q < frames // 8:
                        accs[j - q] = accs[j - q] + spread[q] * tile
        for j, acc in enumerate(accs):
            conv[8 * j : 8 * j + 8, cols] = acc

    gain = conv_gain[...]
    bias = conv_bias[...]
    sum_gain = jnp.zeros((8, channels), F32)
    sum_bias = jnp.zeros((8, channels), F32)
    for r in range(0, frames, 16):
        z = conv[r : r + 16, :]
        z = z - row_mean(z)
        inv = lax.rsqrt(row_mean(z * z) + EPSILON)
        z = z * inv
        act_in = z * gain + bias
        sig = jax.nn.sigmoid(act_in)
        act = act_in * sig
        act_out[r : r + 16, :] = act.astype(BF16)
        d_act = cotangent[r : r + 16, :].astype(F32) * (sig + act * (1.0 - sig))
        d_gain = d_act * z
        sum_gain = sum_gain + d_gain[:8] + d_gain[8:]
        sum_bias = sum_bias + d_act[:8] + d_act[8:]
        g = d_act * gain
        d = (inv * (g - row_mean(g) - z * row_mean(g * z))).astype(BF16).astype(F32)
        for c in range(channels // LANES):
            d_conv[c, r : r + 16, :] = d[:, c * LANES : (c + 1) * LANES]
    write = pltpu.make_async_copy(act_out, conv_act, sem)
    write.start()
    pack[n_taps : n_taps + 1, :] = jnp.sum(sum_gain, axis=0, keepdims=True)
    pack[n_taps + 1 : n_taps + 2, :] = jnp.sum(sum_bias, axis=0, keepdims=True)

    for c in range(channels // LANES):
        cols = slice(c * LANES, (c + 1) * LANES)
        d = [d_conv[c, 8 * j : 8 * j + 8, :] for j in range(frames // 8)]
        for at, taps_at in by_offset:
            accs = {q: jnp.zeros((8, LANES), F32) for q, _ in taps_at}
            for j in range(frames // 8 + 3):
                tile = gated[c, pl.ds(8 * j + at, 8), :]
                for q in accs:
                    if 0 <= j - q < frames // 8:
                        accs[q] = accs[q] + d[j - q] * tile
            for q, t in taps_at:
                taps[t * 8 : t * 8 + 8, :] = accs[q]
        total = taps[pl.ds(0, n_taps, stride=8), :]
        for s in range(1, 8):
            total = total + taps[pl.ds(s, n_taps, stride=8), :]
        pack[0:n_taps, cols] = total

    used = n_taps + 2
    if pairwise:
        sums[...] = pack[0:used, :].astype(BF16)
    else:
        sums[...] = pack[0:used, :]
    for target, near in ((to_a, True), (to_b, False)):
        for c in range(channels // LANES):
            tail, head = d_conv[c, frames - rim :, :], d_conv[c, 0:rim, :]
            edge = jnp.where(swap, head, tail) if near else jnp.where(swap, tail, head)
            pack[used : used + rim, c * LANES : (c + 1) * LANES] = edge
        target[...] = pack[...].astype(BF16)
    write.wait()


def back_rows(kernel, gain, w_in, d_conv, left, sig, x_norm, inv_norm, d_glu, d_normed, rows):
    n_taps, channels = kernel.shape
    model = w_in.shape[0]
    for c in range(channels // LANES):
        cols = slice(c * LANES, (c + 1) * LANES)
        acc = jnp.zeros((rows, LANES), F32)
        for t in range(n_taps):
            acc = acc + kernel[t : t + 1, cols] * d_conv(c, t)
        sg = sig(cols)
        d_left = acc * sg
        d_glu[:, cols] = d_left.astype(BF16)
        d_glu[:, channels + c * LANES : channels + (c + 1) * LANES] = (
            d_left * left(cols) * (1.0 - sg)
        ).astype(BF16)
    step = 256
    for n in range(model // step):
        d_normed[:, pl.ds(n * step, step)] = dot_t(d_glu[...], w_in[pl.ds(n * step, step), :])
    for r in range(0, rows, 32):
        g = d_normed[r : r + 32, :] * gain
        x = x_norm(r)
        yield r, (inv_norm(r) * (g - row_mean(g) - x * row_mean(g * x))).astype(BF16)


def inner_kernel(
    kernel, norm_gain, w_in, x_norm, inv_norm, left, sig, d_conv, sums, out, sums_out, d_glu,
    d_normed,
):
    sums_out[...] = sums[...]
    rows = out.shape[0]
    rim = (kernel.shape[0] - 1) // 2
    blocks = back_rows(
        kernel, norm_gain[...], w_in,
        lambda c, t: d_conv[c, pl.ds(HALO + rim - t, rows), :],
        lambda cols: left[HALO : HALO + rows, cols],
        lambda cols: sig[HALO : HALO + rows, cols],
        lambda r: x_norm[2 * HALO + r : 2 * HALO + r + 32, :],
        lambda r: inv_norm[2 * HALO + r : 2 * HALO + r + 32, 0:1],
        d_glu, d_normed, rows,
    )
    for r, block in blocks:
        out[r : r + 32, :] = block


def edge_kernel(
    pairwise, count, inner, from_b, from_a, kernel, norm_gain, w_in, x_norm, inv_norm, left, sig,
    d_conv, d_hidden, padded, edges, d_glu, d_normed, out, sem,
):
    frames, channels = left.shape
    n_taps = kernel.shape[0]
    rim = (n_taps - 1) // 2
    me = lax.axis_index("ctx")
    swap = swapped(pairwise)
    used = n_taps + 2
    writes = [pltpu.make_async_copy(inner, d_hidden.at[pl.ds(HALO, inner.shape[0]), :], sem.at[2])]
    writes[0].start()
    edges[0] = from_a[...].astype(F32)
    edges[1] = from_b[...].astype(F32)
    for c in range(channels // LANES):
        cols = slice(c * LANES, (c + 1) * LANES)
        a, b = edges[0, used : used + rim, cols], edges[1, used : used + rim, cols]
        padded[0, c, HALO - rim : HALO, :] = jnp.where(me == 0, 0.0, jnp.where(swap, a, b))
        padded[0, c, HALO:, :] = d_conv[c, 0 : 2 * HALO, :]
        padded[1, c, 0 : 2 * HALO, :] = d_conv[c, frames - 2 * HALO :, :]
        padded[1, c, 2 * HALO : 2 * HALO + rim, :] = jnp.where(
            me == count - 1, 0.0, jnp.where(swap, b, a)
        )

    def both(ref, at, cols):
        low = ref[at : at + HALO, cols]
        return jnp.concatenate([low, ref[at + frames - HALO : at + frames, cols]], axis=0)

    def pick(c, t):
        rows = pl.ds(HALO + rim - t, HALO)
        return jnp.concatenate([padded[0, c, rows, :], padded[1, c, rows, :]], axis=0)

    every = slice(None)
    blocks = back_rows(
        kernel, norm_gain[...], w_in, pick,
        lambda cols: both(left, 0, cols), lambda cols: both(sig, 0, cols),
        lambda r: both(x_norm, HALO, every), lambda r: both(inv_norm, HALO, slice(0, 1)),
        d_glu, d_normed, 2 * HALO,
    )
    for r, block in blocks:
        out[...] = block
    writes += [
        pltpu.make_async_copy(
            out.at[pl.ds(i * HALO, HALO), :],
            d_hidden.at[pl.ds(i * (frames - HALO), HALO), :],
            sem.at[i],
        )
        for i in range(2)
    ]
    for write in writes[1:]:
        write.start()
    for write in writes:
        write.wait()


def total_kernel(factor, one, two, three, four, d_kernel, d_gain, d_bias):
    n_taps = d_kernel.shape[0]
    total = (one[...].astype(F32) + two[...].astype(F32)) + (
        three[...].astype(F32) + four[...].astype(F32)
    )
    total = total * factor
    d_kernel[...] = total[0:n_taps]
    d_gain[...] = total[n_taps : n_taps + 1]
    d_bias[...] = total[n_taps + 1 :]


def flips(array, axis, which):
    return [lax.ppermute(array, axis, [(i, i ^ k) for i in range(4)]) for k in which]


def to_neighbours(pairwise, count, to_a, to_b):
    if pairwise:
        return flips(to_a, "ctx", (1,)) + flips(to_b, "ctx", (3,))
    return [
        lax.ppermute(to_b, "ctx", [((i + 1) % count, i) for i in range(count)]),
        lax.ppermute(to_a, "ctx", [(i, (i + 1) % count) for i in range(count)]),
    ]


def per_device(
    resid, query, keys, values, w_out, norm_gain, w_in, kernel, conv_gain, conv_bias, cotangent
):
    frames, model = resid.shape[1:]
    width = query.shape[2]
    channels = cotangent.shape[2]
    n_taps = kernel.shape[0]
    rim = (n_taps - 1) // 2
    ctx, dp = lax.axis_size("ctx"), lax.axis_size("dp")
    pairwise = ctx == 4 and dp == 4
    resid, query, keys, values, cotangent = (
        x.reshape(x.shape[1:]) for x in (resid, query, keys, values, cotangent)
    )
    norm_gain, conv_gain, conv_bias = (x.reshape(1, -1) for x in (norm_gain, conv_gain, conv_bias))
    pooled = frames // POOL
    message = 2 * pooled + HALO * (1 + model // width)
    n_edges = 2 * (1 + model // width)

    own, to_a, to_b = pl.pallas_call(
        functools.partial(pack_kernel, pairwise),
        out_shape=(
            shape((2 * pooled, width), BF16),
            shape((message, width), BF16),
            shape((message - 2 * pooled, width), BF16),
        ),
        in_specs=[HBM] * 4,
        out_specs=(VMEM,) * 3,
        scratch_shapes=[
            pltpu.VMEM((2, frames, width), BF16),
            pltpu.SemaphoreType.DMA((n_edges,)),
            pltpu.SemaphoreType.DMA((2,)),
        ],
        compiler_params=pltpu.CompilerParams(vmem_limit_bytes=4 * 2**20),
    )(*in_hbm(keys, values, query, resid))

    if pairwise:
        (from_a,) = flips(to_a, "ctx", (1,))
        far, across = flips(own, "ctx", (2, 3))
        from_b = lax.ppermute(to_b, "ctx", [(1, 2), (2, 1)])
        kvs = (own, far, across)
    else:
        from_a, from_b = to_neighbours(pairwise, ctx, to_a[2 * pooled :], to_b)
        kvs = tuple(
            lax.all_gather(part, "ctx", axis=0, tiled=True) for part in (own[:pooled], own[pooled:])
        )

    operands = (
        query, resid, cotangent, w_out, norm_gain, w_in, kernel, conv_gain, conv_bias,
    )
    operands = pl.pallas_call(
        functools.partial(fetch_kernel, len(operands)),
        out_shape=tuple(shape(x.shape, x.dtype) for x in operands),
        in_specs=[HBM] * (1 + len(operands)),
        out_specs=(VMEM,) * len(operands),
        scratch_shapes=[pltpu.SemaphoreType.DMA((len(operands),))],
        compiler_params=pltpu.CompilerParams(vmem_limit_bytes=8 * 2**20),
    )(own, *in_hbm(*operands))
    norm_gain, w_in, kernel = operands[4:7]

    rows = frames + 2 * HALO
    used = n_taps + 2
    conv_act, x_norm, inv_norm, left, sig, d_conv, to_a, to_b, sums = pl.pallas_call(
        functools.partial(main_kernel, pairwise, ctx, len(kvs)),
        out_shape=(
            shape((frames, channels), BF16),
            shape((rows, model), F32),
            shape((rows, LANES), F32),
            shape((frames, channels), F32),
            shape((frames, channels), F32),
            shape((channels // LANES, frames, LANES), F32),
            shape((used + rim, channels), BF16),
            shape((used + rim, channels), BF16),
            shape((used, channels), BF16 if pairwise else F32),
        ),
        in_specs=[VMEM] * (11 + len(kvs)),
        out_specs=(HBM,) + (VMEM,) * 8,
        scratch_shapes=[
            pltpu.VMEM((rows, width), BF16),
            pltpu.VMEM((2 * HALO, model), BF16),
            pltpu.VMEM((pooled * ctx, width), BF16),
            pltpu.VMEM((pooled * ctx, width), BF16),
            pltpu.VMEM((rows, width), BF16),
            pltpu.VMEM((rows, model), F32),
            pltpu.VMEM((rows, model), BF16),
            pltpu.VMEM((channels // LANES, rows, LANES), F32),
            pltpu.VMEM((frames, channels), F32),
            pltpu.VMEM((channels // LANES, rows, 2 * LANES), F32),
            pltpu.VMEM((n_taps * 8, LANES), F32),
            pltpu.VMEM((frames, channels), BF16),
            pltpu.VMEM((used + rim, channels), F32),
            pltpu.SemaphoreType.DMA,
        ],
        compiler_params=pltpu.CompilerParams(vmem_limit_bytes=32 * 2**20),
    )(*operands, *kvs, from_b, from_a)

    inner = frames - 2 * HALO
    common = (kernel, norm_gain, w_in, x_norm, inv_norm, left, sig, d_conv)
    d_inner, same_sums = pl.pallas_call(
        inner_kernel,
        out_shape=(shape((inner, model), BF16), shape(sums.shape, sums.dtype)),
        in_specs=[VMEM] * 9,
        out_specs=(VMEM, VMEM),
        scratch_shapes=[
            pltpu.VMEM((inner, 2 * channels), BF16),
            pltpu.VMEM((inner, model), F32),
        ],
        compiler_params=pltpu.CompilerParams(vmem_limit_bytes=16 * 2**20),
    )(*common, sums)
    if pairwise:
        (from_b,) = flips(to_b, "ctx", (3,))
        (far,) = flips(sums, "ctx", (2,))
        (from_a,) = flips(to_a, "ctx", (1,))
        near, across = (x[:used].astype(F32) for x in (from_a, from_b))
        sums = ((same_sums.astype(F32) + near) + (far.astype(F32) + across)).astype(BF16)
        parts = [sums] + flips(sums, "dp", (1, 2, 3))
    else:
        from_a, from_b = to_neighbours(pairwise, ctx, to_a, to_b)
        sums = same_sums

    d_hidden = pl.pallas_call(
        functools.partial(edge_kernel, pairwise, ctx),
        out_shape=shape((frames, model), BF16),
        in_specs=[VMEM] * 11,
        out_specs=HBM,
        scratch_shapes=[
            pltpu.VMEM((2, channels // LANES, 3 * HALO, LANES), F32),
            pltpu.VMEM((2, used + rim, channels), F32),
            pltpu.VMEM((2 * HALO, 2 * channels), BF16),
            pltpu.VMEM((2 * HALO, model), F32),
            pltpu.VMEM((2 * HALO, model), BF16),
            pltpu.SemaphoreType.DMA((3,)),
        ],
        compiler_params=pltpu.CompilerParams(vmem_limit_bytes=16 * 2**20),
    )(d_inner, from_b, from_a, *common)

    factor = 1.0 / math.sqrt(frames * ctx * dp)
    if pairwise:
        d_kernel, d_gain, d_bias = pl.pallas_call(
            functools.partial(total_kernel, factor),
            out_shape=(shape((n_taps, channels), F32),) + (shape((1, channels), F32),) * 2,
            in_specs=[VMEM] * 4,
            out_specs=(VMEM,) * 3,
            compiler_params=pltpu.CompilerParams(vmem_limit_bytes=2 * 2**20),
        )(*parts)
        d_gain, d_bias = d_gain.reshape(-1), d_bias.reshape(-1)
    else:
        total = lax.psum(sums, ("ctx", "dp")) * factor
        d_kernel, d_gain, d_bias = total[:n_taps], total[n_taps], total[n_taps + 1]
    return (conv_act[None], d_hidden[None], d_kernel, d_gain, d_bias)


def solution(mesh):
    split = P(("groups", "dp"), "ctx", None)
    return jax.shard_map(
        per_device,
        mesh=mesh,
        in_specs=(split,) * 4 + (P(),) * 6 + (split,),
        out_specs=(split, split, P("groups", None), P("groups"), P("groups")),
        check_vma=False,
    )
```

```python
import functools
import math

import jax
import jax.numpy as jnp
from jax import lax
from jax.experimental import pallas as pl
from jax.experimental.pallas import tpu as pltpu
from jax.sharding import PartitionSpec as P

HEAD_DIM = 64
POOL = 4
EPSILON = 1e-05

LANES = 128
HALO = 16
F32 = jnp.float32
BF16 = jnp.bfloat16

VMEM = pl.BlockSpec(memory_space=pltpu.VMEM)
HBM = pl.BlockSpec(memory_space=pltpu.HBM)
shape = jax.ShapeDtypeStruct


def dot(a, b):
    return lax.dot_general(a, b, (((1,), (0,)), ((), ())), preferred_element_type=F32)


def dot_t(a, b):
    return lax.dot_general(a, b, (((1,), (1,)), ((), ())), preferred_element_type=F32)


def row_mean(x):
    return jnp.sum(x, axis=-1, keepdims=True) * (1.0 / x.shape[-1])


def in_hbm(*arrays):
    return [pltpu.with_memory_space_constraint(x, pltpu.HBM) for x in arrays]


def swapped(pairwise):
    return lax.rem(lax.axis_index("ctx"), 2) == 1 if pairwise else False


def pack_kernel(pairwise, keys, values, query, resid, own, to_a, to_b, kv, sem, kv_sem):
    frames, width = keys.shape
    model = resid.shape[1]
    pooled = frames // POOL
    swap = swapped(pairwise)
    loads = [
        pltpu.make_async_copy(source, kv.at[place], kv_sem.at[place])
        for place, source in enumerate((keys, values))
    ]
    for load in loads:
        load.start()
    edges = []
    for target, near in ((to_a, True), (to_b, False)):
        at = 2 * pooled if near else 0
        start = jnp.where(swap, 0 if near else frames - HALO, frames - HALO if near else 0)
        start = pl.multiple_of(start.astype(jnp.int32), HALO)
        for source, column in [(query, 0)] + [(resid, c) for c in range(0, model, width)]:
            edges.append(
                pltpu.make_async_copy(
                    source.at[pl.ds(start, HALO), pl.ds(column, width)],
                    target.at[pl.ds(at, HALO), :],
                    sem.at[len(edges)],
                )
            )
            edges[-1].start()
            at += HALO
    row = lax.broadcasted_iota(jnp.int32, (pooled, frames), 0)
    col = lax.broadcasted_iota(jnp.int32, (pooled, frames), 1)
    mean = jnp.where(col // POOL == row, 1.0 / POOL, 0.0).astype(BF16)
    for place, load in enumerate(loads):
        load.wait()
        block = dot(mean, kv[place]).astype(BF16)
        rows = pl.ds(place * pooled, pooled)
        own[rows, :] = block
        to_a[rows, :] = block
    for edge in edges:
        edge.wait()


def fetch_kernel(count, after, *refs):
    sources, targets, sem = refs[:count], refs[count : 2 * count], refs[2 * count]
    copies = [
        pltpu.make_async_copy(a, b, sem.at[i]) for i, (a, b) in enumerate(zip(sources, targets))
    ]
    for copy in copies:
        copy.start()
    for copy in copies:
        copy.wait()


def main_kernel(pairwise, count, n_kv, *refs):
    (query, resid, cotangent, w_out, norm_gain, w_in, kernel, conv_gain, conv_bias) = refs[:9]
    kvs = refs[9 : 9 + n_kv]
    from_b, from_a = refs[9 + n_kv : 11 + n_kv]
    (conv_act, x_norm, inv_norm, left_out, sig_out, d_conv) = refs[11 + n_kv : 17 + n_kv]
    to_a, to_b, sums = refs[17 + n_kv : 20 + n_kv]
    (q_all, r_edge, k_all, v_all, att, hid, normed, gated, conv, glu, taps, act_out, pack, sem) = (
        refs[20 + n_kv :]
    )
    frames, width = query.shape
    model = resid.shape[1]
    channels = w_in.shape[1] // 2
    rows = frames + 2 * HALO
    n_taps = kernel.shape[0]
    rim = (n_taps - 1) // 2
    me = lax.axis_index("ctx")
    first = me == 0
    last = me == count - 1
    swap = swapped(pairwise)
    main = pl.ds(HALO, frames)

    pooled = frames // POOL
    if pairwise:
        own, across, far = kvs
        for side, target in enumerate((k_all, v_all)):
            rows_in = pl.ds(side * pooled, pooled)
            target[0:pooled, :] = own[rows_in, :]
            target[pooled : 2 * pooled, :] = from_a[rows_in, :]
            target[2 * pooled : 3 * pooled, :] = far[rows_in, :]
            target[3 * pooled :, :] = across[rows_in, :]
    else:
        for source, target in zip(kvs, (k_all, v_all)):
            target[...] = source[...]
    keylen = count * pooled
    q_all[main, :] = query[...]
    at_a = 2 * pooled if pairwise else 0
    for left_side in (True, False):
        edge_rows = pl.ds(0 if left_side else HALO + frames, HALO)
        r_rows = pl.ds(0 if left_side else HALO, HALO)

        def pick(start):
            a = from_a[pl.ds(at_a + start, HALO), :]
            b = from_b[pl.ds(start, HALO), :]
            return jnp.where(swap, a, b) if left_side else jnp.where(swap, b, a)

        q_all[edge_rows, :] = pick(0)
        for piece in range(model // width):
            r_edge[r_rows, pl.ds(piece * width, width)] = pick(HALO * (1 + piece))

    lane = lax.broadcasted_iota(jnp.int32, (keylen, LANES), 1)
    low = lane < HEAD_DIM
    zero = jnp.zeros((keylen, LANES), BF16)
    ones_low = jnp.where(low, 1.0, 0.0).astype(BF16)
    ones_high = jnp.where(low, 0.0, 1.0).astype(BF16)
    scale = 1.0 / math.sqrt(HEAD_DIM)
    pairs = width // LANES

    def score(pair):
        cols = pl.ds(pair * LANES, LANES)
        k_pair = k_all[:, cols]
        k_both = jnp.concatenate([jnp.where(low, k_pair, zero), jnp.where(low, zero, k_pair)], axis=0)
        return dot_t(q_all[:, cols], k_both)

    upcoming = score(0)
    for pair in range(pairs):
        cols = pl.ds(pair * LANES, LANES)
        scores = upcoming
        if pair + 1 < pairs:
            upcoming = score(pair + 1)
        v_pair = v_all[:, cols]
        probs = []
        for half in (scores[:, :keylen], scores[:, keylen:]):
            top = jnp.max(half, axis=-1, keepdims=True)
            probs.append(jnp.exp((half - top) * scale).astype(BF16))
        v_both = jnp.concatenate(
            [
                jnp.concatenate([jnp.where(low, v_pair, zero), ones_low], axis=1),
                jnp.concatenate([jnp.where(low, zero, v_pair), ones_high], axis=1),
            ],
            axis=0,
        )
        weighted = dot(jnp.concatenate(probs, axis=1), v_both)
        att[:, cols] = (weighted[:, :LANES] / weighted[:, LANES:]).astype(BF16)

    step = 256
    for n in range(model // step):
        cols = pl.ds(n * step, step)
        out = dot(att[...], w_out[:, cols])
        for rows_in, res in (
            (slice(0, HALO), r_edge[0:HALO, cols]),
            (slice(HALO, HALO + frames), resid[:, cols]),
            (slice(HALO + frames, rows), r_edge[HALO:, cols]),
        ):
            hid[rows_in, cols] = (res.astype(F32) + out[rows_in]).astype(BF16).astype(F32)

    gain = norm_gain[...]
    for r in range(0, rows, 16):
        x = hid[r : r + 16, :]
        x = x - row_mean(x)
        inv = lax.rsqrt(row_mean(x * x) + EPSILON)
        x = x * inv
        normed[r : r + 16, :] = (x * gain).astype(BF16)
        x_norm[r : r + 16, :] = x
        inv_norm[r : r + 16, :] = jnp.broadcast_to(inv, (16, LANES))

    def project(c):
        pair = [w_in[:, at + c * LANES : at + (c + 1) * LANES] for at in (0, channels)]
        glu[c] = dot(normed[...], jnp.concatenate(pair, axis=1))

    offsets = [divmod(HALO + t - rim, 8) for t in range(n_taps)]
    by_offset = [
        (at, [(q, t) for t, (q, s) in enumerate(offsets) if s == at]) for at in range(8)
    ]
    project(0)
    for c in range(channels // LANES):
        cols = slice(c * LANES, (c + 1) * LANES)
        if (c + 1) * LANES < channels:
            project(c + 1)
        for r in range(0, rows, 16):
            left = glu[c, r : r + 16, 0:LANES]
            sig = jax.nn.sigmoid(glu[c, r : r + 16, LANES:])
            out = (left * sig).astype(BF16).astype(F32)
            if r < HALO:
                out = jnp.where(first, 0.0, out)
            elif r >= HALO + frames:
                out = jnp.where(last, 0.0, out)
            else:
                left_out[r - HALO : r - HALO + 16, cols] = left
                sig_out[r - HALO : r - HALO + 16, cols] = sig
            gated[c, r : r + 16, :] = out
        accs = [jnp.zeros((8, LANES), F32) for _ in range(frames // 8)]
        for at, taps_at in by_offset:
            spread = {q: jnp.broadcast_to(kernel[t : t + 1, cols], (8, LANES)) for q, t in taps_at}
            for j in range(frames // 8 + 3):
                tile = gated[c, pl.ds(8 * j + at, 8), :]
                for q, _ in taps_at:
                    if 0 <= j - q < frames // 8:
                        accs[j - q] = accs[j - q] + spread[q] * tile
        for j, acc in enumerate(accs):
            conv[8 * j : 8 * j + 8, cols] = acc

    gain = conv_gain[...]
    bias = conv_bias[...]
    sum_gain = jnp.zeros((8, channels), F32)
    sum_bias = jnp.zeros((8, channels), F32)
    for r in range(0, frames, 16):
        z = conv[r : r + 16, :]
        z = z - row_mean(z)
        inv = lax.rsqrt(row_mean(z * z) + EPSILON)
        z = z * inv
        act_in = z * gain + bias
        sig = jax.nn.sigmoid(act_in)
        act = act_in * sig
        act_out[r : r + 16, :] = act.astype(BF16)
        d_act = cotangent[r : r + 16, :].astype(F32) * (sig + act * (1.0 - sig))
        d_gain = d_act * z
        sum_gain = sum_gain + d_gain[:8] + d_gain[8:]
        sum_bias = sum_bias + d_act[:8] + d_act[8:]
        g = d_act * gain
        d = (inv * (g - row_mean(g) - z * row_mean(g * z))).astype(BF16).astype(F32)
        for c in range(channels // LANES):
            d_conv[c, r : r + 16, :] = d[:, c * LANES : (c + 1) * LANES]
    write = pltpu.make_async_copy(act_out, conv_act, sem)
    write.start()
    pack[n_taps : n_taps + 1, :] = jnp.sum(sum_gain, axis=0, keepdims=True)
    pack[n_taps + 1 : n_taps + 2, :] = jnp.sum(sum_bias, axis=0, keepdims=True)

    for c in range(channels // LANES):
        cols = slice(c * LANES, (c + 1) * LANES)
        d = [d_conv[c, 8 * j : 8 * j + 8, :] for j in range(frames // 8)]
        for at, taps_at in by_offset:
            accs = {q: jnp.zeros((8, LANES), F32) for q, _ in taps_at}
            for j in range(frames // 8 + 3):
                tile = gated[c, pl.ds(8 * j + at, 8), :]
                for q in accs:
                    if 0 <= j - q < frames // 8:
                        accs[q] = accs[q] + d[j - q] * tile
            for q, t in taps_at:
                taps[t * 8 : t * 8 + 8, :] = accs[q]
        total = taps[pl.ds(0, n_taps, stride=8), :]
        for s in range(1, 8):
            total = total + taps[pl.ds(s, n_taps, stride=8), :]
        pack[0:n_taps, cols] = total

    used = n_taps + 2
    if pairwise:
        sums[...] = pack[0:used, :].astype(BF16)
    else:
        sums[...] = pack[0:used, :]
    for target, near in ((to_a, True), (to_b, False)):
        for c in range(channels // LANES):
            tail, head = d_conv[c, frames - rim :, :], d_conv[c, 0:rim, :]
            edge = jnp.where(swap, head, tail) if near else jnp.where(swap, tail, head)
            pack[used : used + rim, c * LANES : (c + 1) * LANES] = edge
        target[...] = pack[...].astype(BF16)
    write.wait()


def back_rows(kernel, gain, w_in, d_conv, left, sig, x_norm, inv_norm, d_glu, d_normed, rows):
    n_taps, channels = kernel.shape
    model = w_in.shape[0]
    for c in range(channels // LANES):
        cols = slice(c * LANES, (c + 1) * LANES)
        acc = jnp.zeros((rows, LANES), F32)
        for t in range(n_taps):
            acc = acc + kernel[t : t + 1, cols] * d_conv(c, t)
        sg = sig(cols)
        d_left = acc * sg
        d_glu[:, cols] = d_left.astype(BF16)
        d_glu[:, channels + c * LANES : channels + (c + 1) * LANES] = (
            d_left * left(cols) * (1.0 - sg)
        ).astype(BF16)
    step = 256
    for n in range(model // step):
        d_normed[:, pl.ds(n * step, step)] = dot_t(d_glu[...], w_in[pl.ds(n * step, step), :])
    for r in range(0, rows, 32):
        g = d_normed[r : r + 32, :] * gain
        x = x_norm(r)
        yield r, (inv_norm(r) * (g - row_mean(g) - x * row_mean(g * x))).astype(BF16)


def inner_kernel(
    kernel, norm_gain, w_in, x_norm, inv_norm, left, sig, d_conv, sums, out, sums_out, d_glu,
    d_normed,
):
    sums_out[...] = sums[...]
    rows = out.shape[0]
    rim = (kernel.shape[0] - 1) // 2
    blocks = back_rows(
        kernel, norm_gain[...], w_in,
        lambda c, t: d_conv[c, pl.ds(HALO + rim - t, rows), :],
        lambda cols: left[HALO : HALO + rows, cols],
        lambda cols: sig[HALO : HALO + rows, cols],
        lambda r: x_norm[2 * HALO + r : 2 * HALO + r + 32, :],
        lambda r: inv_norm[2 * HALO + r : 2 * HALO + r + 32, 0:1],
        d_glu, d_normed, rows,
    )
    for r, block in blocks:
        out[r : r + 32, :] = block


def edge_kernel(
    pairwise, count, inner, from_b, from_a, kernel, norm_gain, w_in, x_norm, inv_norm, left, sig,
    d_conv, d_hidden, padded, edges, d_glu, d_normed, out, sem,
):
    frames, channels = left.shape
    n_taps = kernel.shape[0]
    rim = (n_taps - 1) // 2
    me = lax.axis_index("ctx")
    swap = swapped(pairwise)
    used = n_taps + 2
    writes = [pltpu.make_async_copy(inner, d_hidden.at[pl.ds(HALO, inner.shape[0]), :], sem.at[2])]
    writes[0].start()
    edges[0] = from_a[...].astype(F32)
    edges[1] = from_b[...].astype(F32)
    for c in range(channels // LANES):
        cols = slice(c * LANES, (c + 1) * LANES)
        a, b = edges[0, used : used + rim, cols], edges[1, used : used + rim, cols]
        padded[0, c, HALO - rim : HALO, :] = jnp.where(me == 0, 0.0, jnp.where(swap, a, b))
        padded[0, c, HALO:, :] = d_conv[c, 0 : 2 * HALO, :]
        padded[1, c, 0 : 2 * HALO, :] = d_conv[c, frames - 2 * HALO :, :]
        padded[1, c, 2 * HALO : 2 * HALO + rim, :] = jnp.where(
            me == count - 1, 0.0, jnp.where(swap, b, a)
        )

    def both(ref, at, cols):
        low = ref[at : at + HALO, cols]
        return jnp.concatenate([low, ref[at + frames - HALO : at + frames, cols]], axis=0)

    def pick(c, t):
        rows = pl.ds(HALO + rim - t, HALO)
        return jnp.concatenate([padded[0, c, rows, :], padded[1, c, rows, :]], axis=0)

    every = slice(None)
    blocks = back_rows(
        kernel, norm_gain[...], w_in, pick,
        lambda cols: both(left, 0, cols), lambda cols: both(sig, 0, cols),
        lambda r: both(x_norm, HALO, every), lambda r: both(inv_norm, HALO, slice(0, 1)),
        d_glu, d_normed, 2 * HALO,
    )
    for r, block in blocks:
        out[...] = block
    writes += [
        pltpu.make_async_copy(
            out.at[pl.ds(i * HALO, HALO), :],
            d_hidden.at[pl.ds(i * (frames - HALO), HALO), :],
            sem.at[i],
        )
        for i in range(2)
    ]
    for write in writes[1:]:
        write.start()
    for write in writes:
        write.wait()


def total_kernel(factor, one, two, three, four, d_kernel, d_gain, d_bias):
    n_taps = d_kernel.shape[0]
    total = (one[...].astype(F32) + two[...].astype(F32)) + (
        three[...].astype(F32) + four[...].astype(F32)
    )
    total = total * factor
    d_kernel[...] = total[0:n_taps]
    d_gain[...] = total[n_taps : n_taps + 1]
    d_bias[...] = total[n_taps + 1 :]


def flips(array, axis, which):
    return [lax.ppermute(array, axis, [(i, i ^ k) for i in range(4)]) for k in which]


def to_neighbours(pairwise, count, to_a, to_b):
    if pairwise:
        return flips(to_a, "ctx", (1,)) + flips(to_b, "ctx", (3,))
    return [
        lax.ppermute(to_b, "ctx", [((i + 1) % count, i) for i in range(count)]),
        lax.ppermute(to_a, "ctx", [(i, (i + 1) % count) for i in range(count)]),
    ]


def per_device(
    resid, query, keys, values, w_out, norm_gain, w_in, kernel, conv_gain, conv_bias, cotangent
):
    frames, model = resid.shape[1:]
    width = query.shape[2]
    channels = cotangent.shape[2]
    n_taps = kernel.shape[0]
    rim = (n_taps - 1) // 2
    ctx, dp = lax.axis_size("ctx"), lax.axis_size("dp")
    pairwise = ctx == 4 and dp == 4
    resid, query, keys, values, cotangent = (
        x.reshape(x.shape[1:]) for x in (resid, query, keys, values, cotangent)
    )
    norm_gain, conv_gain, conv_bias = (x.reshape(1, -1) for x in (norm_gain, conv_gain, conv_bias))
    pooled = frames // POOL
    message = 2 * pooled + HALO * (1 + model // width)
    n_edges = 2 * (1 + model // width)

    own, to_a, to_b = pl.pallas_call(
        functools.partial(pack_kernel, pairwise),
        out_shape=(
            shape((2 * pooled, width), BF16),
            shape((message, width), BF16),
            shape((message - 2 * pooled, width), BF16),
        ),
        in_specs=[HBM] * 4,
        out_specs=(VMEM,) * 3,
        scratch_shapes=[
            pltpu.VMEM((2, frames, width), BF16),
            pltpu.SemaphoreType.DMA((n_edges,)),
            pltpu.SemaphoreType.DMA((2,)),
        ],
        compiler_params=pltpu.CompilerParams(vmem_limit_bytes=4 * 2**20),
    )(*in_hbm(keys, values, query, resid))

    if pairwise:
        (from_a,) = flips(to_a, "ctx", (1,))
        far, across = flips(own, "ctx", (2, 3))
        from_b = lax.ppermute(to_b, "ctx", [(1, 2), (2, 1)])
        kvs = (own, across, far)
    else:
        from_a, from_b = to_neighbours(pairwise, ctx, to_a[2 * pooled :], to_b)
        kvs = tuple(
            lax.all_gather(part, "ctx", axis=0, tiled=True) for part in (own[:pooled], own[pooled:])
        )

    operands = (
        query, resid, cotangent, w_out, norm_gain, w_in, kernel, conv_gain, conv_bias,
    )
    operands = pl.pallas_call(
        functools.partial(fetch_kernel, len(operands)),
        out_shape=tuple(shape(x.shape, x.dtype) for x in operands),
        in_specs=[HBM] * (1 + len(operands)),
        out_specs=(VMEM,) * len(operands),
        scratch_shapes=[pltpu.SemaphoreType.DMA((len(operands),))],
        compiler_params=pltpu.CompilerParams(vmem_limit_bytes=8 * 2**20),
    )(own, *in_hbm(*operands))
    norm_gain, w_in, kernel = operands[4:7]

    rows = frames + 2 * HALO
    used = n_taps + 2
    conv_act, x_norm, inv_norm, left, sig, d_conv, to_a, to_b, sums = pl.pallas_call(
        functools.partial(main_kernel, pairwise, ctx, len(kvs)),
        out_shape=(
            shape((frames, channels), BF16),
            shape((rows, model), F32),
            shape((rows, LANES), F32),
            shape((frames, channels), F32),
            shape((frames, channels), F32),
            shape((channels // LANES, frames, LANES), F32),
            shape((used + rim, channels), BF16),
            shape((used + rim, channels), BF16),
            shape((used, channels), BF16 if pairwise else F32),
        ),
        in_specs=[VMEM] * (11 + len(kvs)),
        out_specs=(HBM,) + (VMEM,) * 8,
        scratch_shapes=[
            pltpu.VMEM((rows, width), BF16),
            pltpu.VMEM((2 * HALO, model), BF16),
            pltpu.VMEM((pooled * ctx, width), BF16),
            pltpu.VMEM((pooled * ctx, width), BF16),
            pltpu.VMEM((rows, width), BF16),
            pltpu.VMEM((rows, model), F32),
            pltpu.VMEM((rows, model), BF16),
            pltpu.VMEM((channels // LANES, rows, LANES), F32),
            pltpu.VMEM((frames, channels), F32),
            pltpu.VMEM((channels // LANES, rows, 2 * LANES), F32),
            pltpu.VMEM((n_taps * 8, LANES), F32),
            pltpu.VMEM((frames, channels), BF16),
            pltpu.VMEM((used + rim, channels), F32),
            pltpu.SemaphoreType.DMA,
        ],
        compiler_params=pltpu.CompilerParams(vmem_limit_bytes=32 * 2**20),
    )(*operands, *kvs, from_b, from_a)

    inner = frames - 2 * HALO
    common = (kernel, norm_gain, w_in, x_norm, inv_norm, left, sig, d_conv)
    d_inner, same_sums = pl.pallas_call(
        inner_kernel,
        out_shape=(shape((inner, model), BF16), shape(sums.shape, sums.dtype)),
        in_specs=[VMEM] * 9,
        out_specs=(VMEM, VMEM),
        scratch_shapes=[
            pltpu.VMEM((inner, 2 * channels), BF16),
            pltpu.VMEM((inner, model), F32),
        ],
        compiler_params=pltpu.CompilerParams(vmem_limit_bytes=16 * 2**20),
    )(*common, sums)
    if pairwise:
        (from_b,) = flips(to_b, "ctx", (3,))
        (far,) = flips(sums, "ctx", (2,))
        (from_a,) = flips(to_a, "ctx", (1,))
        near, across = (x[:used].astype(F32) for x in (from_a, from_b))
        sums = ((same_sums.astype(F32) + near) + (far.astype(F32) + across)).astype(BF16)
        parts = [sums] + flips(sums, "dp", (1, 2, 3))
    else:
        from_a, from_b = to_neighbours(pairwise, ctx, to_a, to_b)
        sums = same_sums

    d_hidden = pl.pallas_call(
        functools.partial(edge_kernel, pairwise, ctx),
        out_shape=shape((frames, model), BF16),
        in_specs=[VMEM] * 11,
        out_specs=HBM,
        scratch_shapes=[
            pltpu.VMEM((2, channels // LANES, 3 * HALO, LANES), F32),
            pltpu.VMEM((2, used + rim, channels), F32),
            pltpu.VMEM((2 * HALO, 2 * channels), BF16),
            pltpu.VMEM((2 * HALO, model), F32),
            pltpu.VMEM((2 * HALO, model), BF16),
            pltpu.SemaphoreType.DMA((3,)),
        ],
        compiler_params=pltpu.CompilerParams(vmem_limit_bytes=16 * 2**20),
    )(d_inner, from_b, from_a, *common)

    factor = 1.0 / math.sqrt(frames * ctx * dp)
    if pairwise:
        d_kernel, d_gain, d_bias = pl.pallas_call(
            functools.partial(total_kernel, factor),
            out_shape=(shape((n_taps, channels), F32),) + (shape((1, channels), F32),) * 2,
            in_specs=[VMEM] * 4,
            out_specs=(VMEM,) * 3,
            compiler_params=pltpu.CompilerParams(vmem_limit_bytes=2 * 2**20),
        )(*parts)
        d_gain, d_bias = d_gain.reshape(-1), d_bias.reshape(-1)
    else:
        total = lax.psum(sums, ("ctx", "dp")) * factor
        d_kernel, d_gain, d_bias = total[:n_taps], total[n_taps], total[n_taps + 1]
    return (conv_act[None], d_hidden[None], d_kernel, d_gain, d_bias)


def solution(mesh):
    split = P(("groups", "dp"), "ctx", None)
    return jax.shard_map(
        per_device,
        mesh=mesh,
        in_specs=(split,) * 4 + (P(),) * 6 + (split,),
        out_specs=(split, split, P("groups", None), P("groups"), P("groups")),
        check_vma=False,
    )
```

```python
import functools
import math

import jax
import jax.numpy as jnp
from jax import lax
from jax.experimental import pallas as pl
from jax.experimental.pallas import tpu as pltpu
from jax.sharding import PartitionSpec as P

HEAD_DIM = 64
POOL = 4
EPSILON = 1e-05

LANES = 128
HALO = 16
F32 = jnp.float32
BF16 = jnp.bfloat16

VMEM = pl.BlockSpec(memory_space=pltpu.VMEM)
HBM = pl.BlockSpec(memory_space=pltpu.HBM)
shape = jax.ShapeDtypeStruct


def dot(a, b):
    return lax.dot_general(a, b, (((1,), (0,)), ((), ())), preferred_element_type=F32)


def dot_t(a, b):
    return lax.dot_general(a, b, (((1,), (1,)), ((), ())), preferred_element_type=F32)


def row_mean(x):
    return jnp.sum(x, axis=-1, keepdims=True) * (1.0 / x.shape[-1])


def in_hbm(*arrays):
    return [pltpu.with_memory_space_constraint(x, pltpu.HBM) for x in arrays]


def swapped(pairwise):
    return lax.rem(lax.axis_index("ctx"), 2) == 1 if pairwise else False


def pack_kernel(pairwise, keys, values, query, resid, own, to_a, to_b, kv, sem, kv_sem):
    frames, width = keys.shape
    model = resid.shape[1]
    pooled = frames // POOL
    swap = swapped(pairwise)
    loads = [
        pltpu.make_async_copy(source, kv.at[place], kv_sem.at[place])
        for place, source in enumerate((keys, values))
    ]
    for load in loads:
        load.start()
    edges = []
    for target, near in ((to_a, True), (to_b, False)):
        at = 2 * pooled if near else 0
        start = jnp.where(swap, 0 if near else frames - HALO, frames - HALO if near else 0)
        start = pl.multiple_of(start.astype(jnp.int32), HALO)
        for source, column in [(query, 0)] + [(resid, c) for c in range(0, model, width)]:
            edges.append(
                pltpu.make_async_copy(
                    source.at[pl.ds(start, HALO), pl.ds(column, width)],
                    target.at[pl.ds(at, HALO), :],
                    sem.at[len(edges)],
                )
            )
            edges[-1].start()
            at += HALO
    row = lax.broadcasted_iota(jnp.int32, (pooled, frames), 0)
    col = lax.broadcasted_iota(jnp.int32, (pooled, frames), 1)
    mean = jnp.where(col // POOL == row, 1.0 / POOL, 0.0).astype(BF16)
    for place, load in enumerate(loads):
        load.wait()
        block = dot(mean, kv[place]).astype(BF16)
        rows = pl.ds(place * pooled, pooled)
        own[rows, :] = block
        to_a[rows, :] = block
    for edge in edges:
        edge.wait()


def fetch_kernel(count, after, *refs):
    sources, targets, sem = refs[:count], refs[count : 2 * count], refs[2 * count]
    copies = [
        pltpu.make_async_copy(a, b, sem.at[i]) for i, (a, b) in enumerate(zip(sources, targets))
    ]
    for copy in copies:
        copy.start()
    for copy in copies:
        copy.wait()


def main_kernel(pairwise, count, n_kv, *refs):
    (query, resid, cotangent, w_out, norm_gain, w_in, kernel, conv_gain, conv_bias) = refs[:9]
    kvs = refs[9 : 9 + n_kv]
    from_b, from_a = refs[9 + n_kv : 11 + n_kv]
    (conv_act, x_norm, inv_norm, left_out, sig_out, d_conv) = refs[11 + n_kv : 17 + n_kv]
    to_a, to_b, sums = refs[17 + n_kv : 20 + n_kv]
    (q_all, r_edge, k_all, v_all, att, hid, normed, gated, conv, glu, taps, act_out, pack, lines, sem) = (
        refs[20 + n_kv :]
    )
    frames, width = query.shape
    model = resid.shape[1]
    channels = w_in.shape[1] // 2
    rows = frames + 2 * HALO
    n_taps = kernel.shape[0]
    rim = (n_taps - 1) // 2
    me = lax.axis_index("ctx")
    first = me == 0
    last = me == count - 1
    swap = swapped(pairwise)
    main = pl.ds(HALO, frames)

    pooled = frames // POOL
    if pairwise:
        own, across, far = kvs
        for side, target in enumerate((k_all, v_all)):
            rows_in = pl.ds(side * pooled, pooled)
            target[0:pooled, :] = own[rows_in, :]
            target[pooled : 2 * pooled, :] = from_a[rows_in, :]
            target[2 * pooled : 3 * pooled, :] = far[rows_in, :]
            target[3 * pooled :, :] = across[rows_in, :]
    else:
        for source, target in zip(kvs, (k_all, v_all)):
            target[...] = source[...]
    keylen = count * pooled
    q_all[main, :] = query[...]
    at_a = 2 * pooled if pairwise else 0
    for left_side in (True, False):
        edge_rows = pl.ds(0 if left_side else HALO + frames, HALO)
        r_rows = pl.ds(0 if left_side else HALO, HALO)

        def pick(start):
            a = from_a[pl.ds(at_a + start, HALO), :]
            b = from_b[pl.ds(start, HALO), :]
            return jnp.where(swap, a, b) if left_side else jnp.where(swap, b, a)

        q_all[edge_rows, :] = pick(0)
        for piece in range(model // width):
            r_edge[r_rows, pl.ds(piece * width, width)] = pick(HALO * (1 + piece))

    lane = lax.broadcasted_iota(jnp.int32, (keylen, LANES), 1)
    low = lane < HEAD_DIM
    zero = jnp.zeros((keylen, LANES), BF16)
    ones_low = jnp.where(low, 1.0, 0.0).astype(BF16)
    ones_high = jnp.where(low, 0.0, 1.0).astype(BF16)
    scale = 1.0 / math.sqrt(HEAD_DIM)
    pairs = width // LANES

    def score(pair):
        cols = pl.ds(pair * LANES, LANES)
        k_pair = k_all[:, cols]
        k_both = jnp.concatenate([jnp.where(low, k_pair, zero), jnp.where(low, zero, k_pair)], axis=0)
        return dot_t(q_all[:, cols], k_both)

    upcoming = score(0)
    for pair in range(pairs):
        cols = pl.ds(pair * LANES, LANES)
        scores = upcoming
        if pair + 1 < pairs:
            upcoming = score(pair + 1)
        v_pair = v_all[:, cols]
        probs = []
        for half in (scores[:, :keylen], scores[:, keylen:]):
            top = jnp.max(half, axis=-1, keepdims=True)
            probs.append(jnp.exp((half - top) * scale).astype(BF16))
        v_both = jnp.concatenate(
            [
                jnp.concatenate([jnp.where(low, v_pair, zero), ones_low], axis=1),
                jnp.concatenate([jnp.where(low, zero, v_pair), ones_high], axis=1),
            ],
            axis=0,
        )
        weighted = dot(jnp.concatenate(probs, axis=1), v_both)
        att[:, cols] = (weighted[:, :LANES] / weighted[:, LANES:]).astype(BF16)

    step = 256
    for n in range(model // step):
        cols = pl.ds(n * step, step)
        out = dot(att[...], w_out[:, cols])
        for rows_in, res in (
            (slice(0, HALO), r_edge[0:HALO, cols]),
            (slice(HALO, HALO + frames), resid[:, cols]),
            (slice(HALO + frames, rows), r_edge[HALO:, cols]),
        ):
            hid[rows_in, cols] = (res.astype(F32) + out[rows_in]).astype(BF16).astype(F32)

    gain = norm_gain[...]
    for r in range(0, rows, 16):
        x = hid[r : r + 16, :]
        x = x - row_mean(x)
        inv = lax.rsqrt(row_mean(x * x) + EPSILON)
        x = x * inv
        normed[r : r + 16, :] = (x * gain).astype(BF16)
        x_norm[r : r + 16, :] = x
        inv_norm[r : r + 16, :] = jnp.broadcast_to(inv, (16, LANES))

    def project(c):
        pair = [w_in[:, at + c * LANES : at + (c + 1) * LANES] for at in (0, channels)]
        glu[c] = dot(normed[...], jnp.concatenate(pair, axis=1))

    offsets = [divmod(HALO + t - rim, 8) for t in range(n_taps)]
    by_offset = [
        (at, [(q, t) for t, (q, s) in enumerate(offsets) if s == at]) for at in range(8)
    ]
    project(0)
    for c in range(channels // LANES):
        cols = slice(c * LANES, (c + 1) * LANES)
        if (c + 1) * LANES < channels:
            project(c + 1)
        for r in range(0, rows, 16):
            left = glu[c, r : r + 16, 0:LANES]
            sig = jax.nn.sigmoid(glu[c, r : r + 16, LANES:])
            out = (left * sig).astype(BF16).astype(F32)
            if r < HALO:
                out = jnp.where(first, 0.0, out)
            elif r >= HALO + frames:
                out = jnp.where(last, 0.0, out)
            else:
                left_out[r - HALO : r - HALO + 16, cols] = left
                sig_out[r - HALO : r - HALO + 16, cols] = sig
            gated[c, r : r + 16, :] = out
        accs = [jnp.zeros((8, LANES), F32) for _ in range(frames // 8)]
        for at, taps_at in by_offset:
            spread = {q: jnp.broadcast_to(kernel[t : t + 1, cols], (8, LANES)) for q, t in taps_at}
            for j in range(frames // 8 + 3):
                tile = gated[c, pl.ds(8 * j + at, 8), :]
                for q, _ in taps_at:
                    if 0 <= j - q < frames // 8:
                        accs[j - q] = accs[j - q] + spread[q] * tile
        for j, acc in enumerate(accs):
            conv[8 * j : 8 * j + 8, cols] = acc

    gain = conv_gain[...]
    bias = conv_bias[...]
    sum_gain = jnp.zeros((8, channels), F32)
    sum_bias = jnp.zeros((8, channels), F32)
    for r in range(0, frames, 16):
        z = conv[r : r + 16, :]
        z = z - row_mean(z)
        inv = lax.rsqrt(row_mean(z * z) + EPSILON)
        z = z * inv
        act_in = z * gain + bias
        sig = jax.nn.sigmoid(act_in)
        act = act_in * sig
        act_out[r : r + 16, :] = act.astype(BF16)
        d_act = cotangent[r : r + 16, :].astype(F32) * (sig + act * (1.0 - sig))
        d_gain = d_act * z
        sum_gain = sum_gain + d_gain[:8] + d_gain[8:]
        sum_bias = sum_bias + d_act[:8] + d_act[8:]
        g = d_act * gain
        d = (inv * (g - row_mean(g) - z * row_mean(g * z))).astype(BF16).astype(F32)
        for c in range(channels // LANES):
            d_conv[c, r : r + 16, :] = d[:, c * LANES : (c + 1) * LANES]
    write = pltpu.make_async_copy(act_out, conv_act, sem)
    write.start()
    pack[n_taps : n_taps + 1, :] = jnp.sum(sum_gain, axis=0, keepdims=True)
    pack[n_taps + 1 : n_taps + 2, :] = jnp.sum(sum_bias, axis=0, keepdims=True)

    for c in range(channels // LANES):
        cols = slice(c * LANES, (c + 1) * LANES)
        d = [d_conv[c, 8 * j : 8 * j + 8, :] for j in range(frames // 8)]
        for at, taps_at in by_offset:
            accs = {q: jnp.zeros((8, LANES), F32) for q, _ in taps_at}
            for j in range(frames // 8 + 3):
                tile = gated[c, pl.ds(8 * j + at, 8), :]
                for q in accs:
                    if 0 <= j - q < frames // 8:
                        accs[q] = accs[q] + d[j - q] * tile
            for q, t in taps_at:
                taps[t * 8 : t * 8 + 8, :] = accs[q]
        total = taps[pl.ds(0, n_taps, stride=8), :]
        for s in range(1, 8):
            total = total + taps[pl.ds(s, n_taps, stride=8), :]
        pack[0:n_taps, cols] = total

    used = n_taps + 2
    blocks = channels // LANES
    for c in range(blocks):
        lines[c * used : (c + 1) * used, :] = pack[0:used, c * LANES : (c + 1) * LANES]
    if pairwise:
        sums[...] = lines[0 : blocks * used, :].astype(BF16)
    else:
        sums[...] = pack[0:used, :]
    for target, near in ((to_a, True), (to_b, False)):
        for c in range(blocks):
            tail, head = d_conv[c, frames - rim :, :], d_conv[c, 0:rim, :]
            at = blocks * used + c * rim
            lines[at : at + rim, :] = (
                jnp.where(swap, head, tail) if near else jnp.where(swap, tail, head)
            )
        target[...] = lines[...].astype(BF16)
    write.wait()


def back_rows(kernel, gain, w_in, d_conv, left, sig, x_norm, inv_norm, d_glu, d_normed, rows):
    n_taps, channels = kernel.shape
    model = w_in.shape[0]
    for c in range(channels // LANES):
        cols = slice(c * LANES, (c + 1) * LANES)
        acc = jnp.zeros((rows, LANES), F32)
        for t in range(n_taps):
            acc = acc + kernel[t : t + 1, cols] * d_conv(c, t)
        sg = sig(cols)
        d_left = acc * sg
        d_glu[:, cols] = d_left.astype(BF16)
        d_glu[:, channels + c * LANES : channels + (c + 1) * LANES] = (
            d_left * left(cols) * (1.0 - sg)
        ).astype(BF16)
    step = 256
    for n in range(model // step):
        d_normed[:, pl.ds(n * step, step)] = dot_t(d_glu[...], w_in[pl.ds(n * step, step), :])
    for r in range(0, rows, 32):
        g = d_normed[r : r + 32, :] * gain
        x = x_norm(r)
        yield r, (inv_norm(r) * (g - row_mean(g) - x * row_mean(g * x))).astype(BF16)


def inner_kernel(
    kernel, norm_gain, w_in, x_norm, inv_norm, left, sig, d_conv, sums, out, sums_out, d_glu,
    d_normed,
):
    sums_out[...] = sums[...]
    rows = out.shape[0]
    rim = (kernel.shape[0] - 1) // 2
    blocks = back_rows(
        kernel, norm_gain[...], w_in,
        lambda c, t: d_conv[c, pl.ds(HALO + rim - t, rows), :],
        lambda cols: left[HALO : HALO + rows, cols],
        lambda cols: sig[HALO : HALO + rows, cols],
        lambda r: x_norm[2 * HALO + r : 2 * HALO + r + 32, :],
        lambda r: inv_norm[2 * HALO + r : 2 * HALO + r + 32, 0:1],
        d_glu, d_normed, rows,
    )
    for r, block in blocks:
        out[r : r + 32, :] = block


def edge_kernel(
    pairwise, count, inner, from_b, from_a, kernel, norm_gain, w_in, x_norm, inv_norm, left, sig,
    d_conv, d_hidden, padded, edges, d_glu, d_normed, out, sem,
):
    frames, channels = left.shape
    n_taps = kernel.shape[0]
    rim = (n_taps - 1) // 2
    me = lax.axis_index("ctx")
    swap = swapped(pairwise)
    used = n_taps + 2
    writes = [pltpu.make_async_copy(inner, d_hidden.at[pl.ds(HALO, inner.shape[0]), :], sem.at[2])]
    writes[0].start()
    edges[0] = from_a[...].astype(F32)
    edges[1] = from_b[...].astype(F32)
    for c in range(channels // LANES):
        cols = slice(c * LANES, (c + 1) * LANES)
        at = channels // LANES * used + c * rim
        a, b = edges[0, at : at + rim, :], edges[1, at : at + rim, :]
        padded[0, c, HALO - rim : HALO, :] = jnp.where(me == 0, 0.0, jnp.where(swap, a, b))
        padded[0, c, HALO:, :] = d_conv[c, 0 : 2 * HALO, :]
        padded[1, c, 0 : 2 * HALO, :] = d_conv[c, frames - 2 * HALO :, :]
        padded[1, c, 2 * HALO : 2 * HALO + rim, :] = jnp.where(
            me == count - 1, 0.0, jnp.where(swap, b, a)
        )

    def both(ref, at, cols):
        low = ref[at : at + HALO, cols]
        return jnp.concatenate([low, ref[at + frames - HALO : at + frames, cols]], axis=0)

    def pick(c, t):
        rows = pl.ds(HALO + rim - t, HALO)
        return jnp.concatenate([padded[0, c, rows, :], padded[1, c, rows, :]], axis=0)

    every = slice(None)
    blocks = back_rows(
        kernel, norm_gain[...], w_in, pick,
        lambda cols: both(left, 0, cols), lambda cols: both(sig, 0, cols),
        lambda r: both(x_norm, HALO, every), lambda r: both(inv_norm, HALO, slice(0, 1)),
        d_glu, d_normed, 2 * HALO,
    )
    for r, block in blocks:
        out[...] = block
    writes += [
        pltpu.make_async_copy(
            out.at[pl.ds(i * HALO, HALO), :],
            d_hidden.at[pl.ds(i * (frames - HALO), HALO), :],
            sem.at[i],
        )
        for i in range(2)
    ]
    for write in writes[1:]:
        write.start()
    for write in writes:
        write.wait()


def total_kernel(factor, one, two, three, four, d_kernel, d_gain, d_bias):
    n_taps = d_kernel.shape[0]
    total = (one[...].astype(F32) + two[...].astype(F32)) + (
        three[...].astype(F32) + four[...].astype(F32)
    )
    total = total * factor
    used = n_taps + 2
    for c in range(d_kernel.shape[1] // LANES):
        cols = slice(c * LANES, (c + 1) * LANES)
        d_kernel[:, cols] = total[c * used : c * used + n_taps]
        d_gain[:, cols] = total[c * used + n_taps : c * used + n_taps + 1]
        d_bias[:, cols] = total[c * used + n_taps + 1 : c * used + n_taps + 2]


def flips(array, axis, which):
    return [lax.ppermute(array, axis, [(i, i ^ k) for i in range(4)]) for k in which]


def to_neighbours(pairwise, count, to_a, to_b):
    if pairwise:
        return flips(to_a, "ctx", (1,)) + flips(to_b, "ctx", (3,))
    return [
        lax.ppermute(to_b, "ctx", [((i + 1) % count, i) for i in range(count)]),
        lax.ppermute(to_a, "ctx", [(i, (i + 1) % count) for i in range(count)]),
    ]


def per_device(
    resid, query, keys, values, w_out, norm_gain, w_in, kernel, conv_gain, conv_bias, cotangent
):
    frames, model = resid.shape[1:]
    width = query.shape[2]
    channels = cotangent.shape[2]
    n_taps = kernel.shape[0]
    rim = (n_taps - 1) // 2
    ctx, dp = lax.axis_size("ctx"), lax.axis_size("dp")
    pairwise = ctx == 4 and dp == 4
    resid, query, keys, values, cotangent = (
        x.reshape(x.shape[1:]) for x in (resid, query, keys, values, cotangent)
    )
    norm_gain, conv_gain, conv_bias = (x.reshape(1, -1) for x in (norm_gain, conv_gain, conv_bias))
    pooled = frames // POOL
    message = 2 * pooled + HALO * (1 + model // width)
    n_edges = 2 * (1 + model // width)

    own, to_a, to_b = pl.pallas_call(
        functools.partial(pack_kernel, pairwise),
        out_shape=(
            shape((2 * pooled, width), BF16),
            shape((message, width), BF16),
            shape((message - 2 * pooled, width), BF16),
        ),
        in_specs=[HBM] * 4,
        out_specs=(VMEM,) * 3,
        scratch_shapes=[
            pltpu.VMEM((2, frames, width), BF16),
            pltpu.SemaphoreType.DMA((n_edges,)),
            pltpu.SemaphoreType.DMA((2,)),
        ],
        compiler_params=pltpu.CompilerParams(vmem_limit_bytes=4 * 2**20),
    )(*in_hbm(keys, values, query, resid))

    if pairwise:
        (from_a,) = flips(to_a, "ctx", (1,))
        far, across = flips(own, "ctx", (2, 3))
        from_b = lax.ppermute(to_b, "ctx", [(1, 2), (2, 1)])
        kvs = (own, across, far)
    else:
        from_a, from_b = to_neighbours(pairwise, ctx, to_a[2 * pooled :], to_b)
        kvs = tuple(
            lax.all_gather(part, "ctx", axis=0, tiled=True) for part in (own[:pooled], own[pooled:])
        )

    operands = (
        query, resid, cotangent, w_out, norm_gain, w_in, kernel, conv_gain, conv_bias,
    )
    operands = pl.pallas_call(
        functools.partial(fetch_kernel, len(operands)),
        out_shape=tuple(shape(x.shape, x.dtype) for x in operands),
        in_specs=[HBM] * (1 + len(operands)),
        out_specs=(VMEM,) * len(operands),
        scratch_shapes=[pltpu.SemaphoreType.DMA((len(operands),))],
        compiler_params=pltpu.CompilerParams(vmem_limit_bytes=8 * 2**20),
    )(own, *in_hbm(*operands))
    norm_gain, w_in, kernel = operands[4:7]

    rows = frames + 2 * HALO
    used = n_taps + 2
    sum_rows = channels // LANES * used
    line_rows = sum_rows + channels // LANES * rim
    conv_act, x_norm, inv_norm, left, sig, d_conv, to_a, to_b, sums = pl.pallas_call(
        functools.partial(main_kernel, pairwise, ctx, len(kvs)),
        out_shape=(
            shape((frames, channels), BF16),
            shape((rows, model), F32),
            shape((rows, LANES), F32),
            shape((frames, channels), F32),
            shape((frames, channels), F32),
            shape((channels // LANES, frames, LANES), F32),
            shape((line_rows, LANES), BF16),
            shape((line_rows, LANES), BF16),
            shape((sum_rows, LANES), BF16) if pairwise else shape((used, channels), F32),
        ),
        in_specs=[VMEM] * (11 + len(kvs)),
        out_specs=(HBM,) + (VMEM,) * 8,
        scratch_shapes=[
            pltpu.VMEM((rows, width), BF16),
            pltpu.VMEM((2 * HALO, model), BF16),
            pltpu.VMEM((pooled * ctx, width), BF16),
            pltpu.VMEM((pooled * ctx, width), BF16),
            pltpu.VMEM((rows, width), BF16),
            pltpu.VMEM((rows, model), F32),
            pltpu.VMEM((rows, model), BF16),
            pltpu.VMEM((channels // LANES, rows, LANES), F32),
            pltpu.VMEM((frames, channels), F32),
            pltpu.VMEM((channels // LANES, rows, 2 * LANES), F32),
            pltpu.VMEM((n_taps * 8, LANES), F32),
            pltpu.VMEM((frames, channels), BF16),
            pltpu.VMEM((used, channels), F32),
            pltpu.VMEM((line_rows, LANES), F32),
            pltpu.SemaphoreType.DMA,
        ],
        compiler_params=pltpu.CompilerParams(vmem_limit_bytes=32 * 2**20),
    )(*operands, *kvs, from_b, from_a)

    inner = frames - 2 * HALO
    common = (kernel, norm_gain, w_in, x_norm, inv_norm, left, sig, d_conv)
    d_inner, same_sums = pl.pallas_call(
        inner_kernel,
        out_shape=(shape((inner, model), BF16), shape(sums.shape, sums.dtype)),
        in_specs=[VMEM] * 9,
        out_specs=(VMEM, VMEM),
        scratch_shapes=[
            pltpu.VMEM((inner, 2 * channels), BF16),
            pltpu.VMEM((inner, model), F32),
        ],
        compiler_params=pltpu.CompilerParams(vmem_limit_bytes=16 * 2**20),
    )(*common, sums)
    if pairwise:
        (from_b,) = flips(to_b, "ctx", (3,))
        (far,) = flips(sums, "ctx", (2,))
        (from_a,) = flips(to_a, "ctx", (1,))
        near, across = (x[:sum_rows].astype(F32) for x in (from_a, from_b))
        sums = ((same_sums.astype(F32) + near) + (far.astype(F32) + across)).astype(BF16)
        parts = [sums] + flips(sums, "dp", (1, 2, 3))
    else:
        from_a, from_b = to_neighbours(pairwise, ctx, to_a, to_b)
        sums = same_sums

    d_hidden = pl.pallas_call(
        functools.partial(edge_kernel, pairwise, ctx),
        out_shape=shape((frames, model), BF16),
        in_specs=[VMEM] * 11,
        out_specs=HBM,
        scratch_shapes=[
            pltpu.VMEM((2, channels // LANES, 3 * HALO, LANES), F32),
            pltpu.VMEM((2, line_rows, LANES), F32),
            pltpu.VMEM((2 * HALO, 2 * channels), BF16),
            pltpu.VMEM((2 * HALO, model), F32),
            pltpu.VMEM((2 * HALO, model), BF16),
            pltpu.SemaphoreType.DMA((3,)),
        ],
        compiler_params=pltpu.CompilerParams(vmem_limit_bytes=16 * 2**20),
    )(d_inner, from_b, from_a, *common)

    factor = 1.0 / math.sqrt(frames * ctx * dp)
    if pairwise:
        d_kernel, d_gain, d_bias = pl.pallas_call(
            functools.partial(total_kernel, factor),
            out_shape=(shape((n_taps, channels), F32),) + (shape((1, channels), F32),) * 2,
            in_specs=[VMEM] * 4,
            out_specs=(VMEM,) * 3,
            compiler_params=pltpu.CompilerParams(vmem_limit_bytes=2 * 2**20),
        )(*parts)
        d_gain, d_bias = d_gain.reshape(-1), d_bias.reshape(-1)
    else:
        total = lax.psum(sums, ("ctx", "dp")) * factor
        d_kernel, d_gain, d_bias = total[:n_taps], total[n_taps], total[n_taps + 1]
    return (conv_act[None], d_hidden[None], d_kernel, d_gain, d_bias)


def solution(mesh):
    split = P(("groups", "dp"), "ctx", None)
    return jax.shard_map(
        per_device,
        mesh=mesh,
        in_specs=(split,) * 4 + (P(),) * 6 + (split,),
        out_specs=(split, split, P("groups", None), P("groups"), P("groups")),
        check_vma=False,
    )
```
